32 devices in a mesh: gx: 4 (over z), gy: 4 (over x, core), gz: 2 (over y).
Axes of the slice: x: 2, y: 2, z: 4, core: 2. Of those that a mesh axis runs over, the one named last changes fastest.
Arguments:
- right_side: float32 [64, 256, 512], P('gx', 'gy', 'gz'), may hold values from -4 to 4
- initial_guess: float32 [64, 256, 512], P('gx', 'gy', 'gz'), may hold values from -3 to 3
- damping: float32 [64, 256, 512], P('gx', 'gy', 'gz'), may hold values from 0.1 to 4
- group_map: int32 [16, 64, 128], P('gx', 'gy', 'gz'), may hold values from 0 to 1023
- block_inverse: float32 [1024, 1024], P('gy'), may hold values from -0.1875 to 0.1875
Outputs:
- fine_iterate: float32 [64, 256, 512], P('gx', 'gy', 'gz')
- middle_correction: float32 [32, 128, 256], P('gx', 'gy', 'gz')
- coarse_correction: float32 [16, 64, 128], P('gx', 'gy', 'gz')
- aggregate_solution: float32 [1024], P('gy')
The draws below stay inside these ranges and needn't reach their ends.
All inputs are finite; a program needn't handle non-finite values.
Results may differ from the reference program's by a relative error of at most 0.0003.
Values sent between devices are 32-bit elements; how exact they have to be, the bound alone decides.
A program may use at most 192 MiB of HBM per device.

```python
import math
import jax
import jax.numpy as jnp
from jax import lax

SWEEPS = 4
NAGG = 1024
NX = 64
NY = 256
NZ = 512
GROUP_CELLS = 128


def draw_right_side(key, part):
    return jax.random.truncated_normal(key, -4.0, 4.0, (NX, NY, NZ), jnp.float32)


def with_ends(result, key, smallest, largest):
    shape = result.shape
    place = [jax.random.randint(jax.random.fold_in(key, axis), (), 0, shape[axis]) for axis in range(len(shape))]
    result = result.at[tuple(place)].set(smallest)
    longest = shape.index(max(shape))
    place[longest] = (place[longest] + 1) % shape[longest]
    return result.at[tuple(place)].set(largest)


def steps_of(key, dims, shards, smallest, top_value):
    def one(axis_at, shards_of):
        steps = jax.random.uniform(jax.random.fold_in(jax.random.fold_in(key, 6), axis_at), (shards_of,), jnp.float32, smallest / len(shards), top_value / len(shards))
        return jnp.repeat(jnp.exp(steps), dims[axis_at] // shards_of).reshape((-1,) + (1,) * (len(dims) - axis_at - 1))

    factor_of = one(*shards[0])
    for cut in shards[1:]:
        factor_of = factor_of * one(*cut)
    return factor_of


def bell_draw(key, extent, scale, reach, shards=(), kind=jnp.bfloat16):
    values = scale * jax.random.normal(key, extent, jnp.float32)
    if shards:
        values = values * steps_of(key, extent, shards, -0.22, 0.18)
    return jnp.clip(values, -reach, reach).astype(kind)


def setup_inputs(seed: int = 0) -> dict:
    streams_of = jax.random.split(jax.random.key(seed), 6)
    right_side = draw_right_side(jax.random.fold_in(streams_of[5], 71), 0)
    initial_guess = bell_draw(streams_of[1], (NX, NY, NZ), 0.5, 3.0, ((0, 4), (1, 4), (2, 2)), jnp.float32)
    damping = jnp.clip(jnp.exp(math.log(4.0) - 3.6888794 * jax.random.uniform(streams_of[2], (NX, NY, NZ), jnp.float32) ** steps_of(streams_of[2], (NX, NY, NZ), ((0, 4), (1, 4), (2, 2)), -0.2, 0.2)), 0.1, 4.0)
    group_map = with_ends(jax.random.randint(streams_of[3], (NX // 4, NY // 4, NZ // 4), 0, NAGG), jax.random.fold_in(streams_of[3], 1), 0, NAGG - 1).astype(jnp.int32)
    block_inverse = bell_draw(streams_of[4], (NAGG, NAGG), NAGG ** -0.5, 0.1875, ((0, 4),), jnp.float32)
    return {"right_side": right_side, "initial_guess": initial_guess, "damping": damping, "group_map": group_map, "block_inverse": block_inverse}


OMEGA = 0.8

def neighbours(padded):
    total = padded[2:, 1:-1, 1:-1] + padded[:-2, 1:-1, 1:-1]
    total = total + padded[1:-1, 2:, 1:-1] + padded[1:-1, :-2, 1:-1]
    return total + padded[1:-1, 1:-1, 2:] + padded[1:-1, 1:-1, :-2]

def relax(padded, source, diagonal):
    centre = padded[1:-1, 1:-1, 1:-1]
    return centre + OMEGA * (source - (diagonal * centre - neighbours(padded))) / diagonal

def defect(padded, source, diagonal):
    centre = padded[1:-1, 1:-1, 1:-1]
    return source - (diagonal * centre - neighbours(padded))

def shrink(field):
    extent_a, extent_b, extent_c = field.shape
    blocks = field.reshape(extent_a // 2, 2, extent_b // 2, 2, extent_c // 2, 2)
    return blocks.sum(axis=(1, 3, 5)) * 0.125

def smooth(start, source, diagonal):
    current = start
    for sweep_count in range(SWEEPS):
        current = relax(jnp.pad(current, 1), source, diagonal)
    return current

def reference(right_side, initial_guess, damping, group_map, block_inverse):
    fine_diag = 6.0 + damping
    fine_iterate = smooth(initial_guess, right_side, fine_diag)
    fine_defect = defect(jnp.pad(fine_iterate, 1), right_side, fine_diag)
    middle_damp = 4.0 * shrink(damping)
    middle_source = 4.0 * shrink(fine_defect)
    middle_diag = 6.0 + middle_damp
    middle = smooth(jnp.zeros_like(middle_source), middle_source, middle_diag)
    middle_defect = defect(jnp.pad(middle, 1), middle_source, middle_diag)
    coarse_damp = 4.0 * shrink(middle_damp)
    coarse_source = 4.0 * shrink(middle_defect)
    coarse_diag = 6.0 + coarse_damp
    coarse = smooth(jnp.zeros_like(coarse_source), coarse_source, coarse_diag)
    coarse_defect = defect(jnp.pad(coarse, 1), coarse_source, coarse_diag)
    summed = jax.ops.segment_sum(coarse_defect.reshape(-1), group_map.reshape(-1), num_segments=NAGG)
    aggregate_source = summed / math.sqrt(GROUP_CELLS)
    solution = jnp.dot(block_inverse, aggregate_source, precision=lax.Precision.HIGHEST)
    return (fine_iterate, middle, coarse, solution)
```

```python
import functools
import math

import jax
import jax.numpy as jnp
from jax import lax
from jax.experimental import pallas as pl
from jax.experimental.pallas import tpu as pltpu
from jax.sharding import PartitionSpec as P

SWEEPS = 4
NAGG = 1024
OMEGA = 0.8
LANES = 128
MESH = pl.DeviceIdType.MESH


def split_dot(left, right_bf16, dims):
    high = left.astype(jnp.bfloat16)
    low = (left - high.astype(jnp.float32)).astype(jnp.bfloat16)
    out = lax.dot_general(high, right_bf16, dims, preferred_element_type=jnp.float32)
    return out + lax.dot_general(low, right_bf16, dims, preferred_element_type=jnp.float32)


def pair_matrix(rows, columns):
    row = lax.broadcasted_iota(jnp.int32, (rows, columns), 0)
    column = lax.broadcasted_iota(jnp.int32, (rows, columns), 1)
    first = jnp.where(row == 2 * column, 1.0, 0.0)
    return (first + jnp.where(row == 2 * column + 1, 1.0, 0.0)).astype(jnp.bfloat16)


class Level:
    def __init__(self, dims, lanes, fields, y_send, y_recv, z_send, z_recv, sems, place, counts):
        self.nx, self.ny, self.nz = dims
        self.lanes = lanes
        self.fields, self.y_send, self.y_recv = fields, y_send, y_recv
        self.z_send, self.z_recv = z_send, z_recv
        self.send_sem, self.recv_sem = sems
        self.gx, self.gy, self.gz = place
        self.counts = counts
        self.edge = jnp.where(self.gz == 0, self.nz - 1, 0)

    def clear(self):
        nx, ny, lanes = self.nx, self.ny, self.lanes
        rounds = self.fields.shape[0]

        @pl.when(self.gx == 0)
        def _():
            for step in range(rounds):
                self.fields[step, 0] = jnp.zeros((ny, lanes), jnp.float32)

        @pl.when(self.gx == self.counts[0] - 1)
        def _():
            for step in range(rounds):
                self.fields[step, nx + 1] = jnp.zeros((ny, lanes), jnp.float32)

        @pl.when(self.gy == 0)
        def _():
            for step in range(rounds):
                self.y_recv[step, 0] = jnp.zeros((nx, lanes), jnp.float32)

        @pl.when(self.gy == self.counts[1] - 1)
        def _():
            for step in range(rounds):
                self.y_recv[step, 1] = jnp.zeros((nx, lanes), jnp.float32)

        for step in range(rounds):
            self.z_send[step] = jnp.zeros((ny, LANES), jnp.float32)

    def x_copies(self, step, low=None, high=None):
        gx, gy, gz = self.gx, self.gy, self.gz
        field = self.fields.at[step]
        low = field.at[1] if low is None else low
        high = field.at[self.nx] if high is None else high
        up = pltpu.make_async_remote_copy(
            src_ref=high, dst_ref=field.at[0],
            send_sem=self.send_sem.at[step, 0], recv_sem=self.recv_sem.at[step, 0],
            device_id=(gx + 1, gy, gz), device_id_type=MESH)
        down = pltpu.make_async_remote_copy(
            src_ref=low, dst_ref=field.at[self.nx + 1],
            send_sem=self.send_sem.at[step, 1], recv_sem=self.recv_sem.at[step, 1],
            device_id=(gx - 1, gy, gz), device_id_type=MESH)
        return (gx, self.counts[0], up, down)

    def y_copies(self, step):
        gx, gy, gz = self.gx, self.gy, self.gz
        up = pltpu.make_async_remote_copy(
            src_ref=self.y_send.at[step, 1], dst_ref=self.y_recv.at[step, 0],
            send_sem=self.send_sem.at[step, 2], recv_sem=self.recv_sem.at[step, 2],
            device_id=(gx, gy + 1, gz), device_id_type=MESH)
        down = pltpu.make_async_remote_copy(
            src_ref=self.y_send.at[step, 0], dst_ref=self.y_recv.at[step, 1],
            send_sem=self.send_sem.at[step, 3], recv_sem=self.recv_sem.at[step, 3],
            device_id=(gx, gy - 1, gz), device_id_type=MESH)
        return (gy, self.counts[1], up, down)

    def z_copy(self, step):
        return pltpu.make_async_remote_copy(
            src_ref=self.z_send.at[step], dst_ref=self.z_recv.at[step],
            send_sem=self.send_sem.at[step, 4], recv_sem=self.recv_sem.at[step, 4],
            device_id=(self.gx, self.gy, 1 - self.gz), device_id_type=MESH)

    @staticmethod
    def start(copies):
        at, count, up, down = copies
        pl.when(at < count - 1)(up.start)
        pl.when(at > 0)(down.start)

    @staticmethod
    def wait_recv(copies):
        at, count, up, down = copies
        pl.when(at > 0)(up.wait_recv)
        pl.when(at < count - 1)(down.wait_recv)

    @staticmethod
    def wait_send(copies):
        at, count, up, down = copies
        pl.when(at < count - 1)(up.wait_send)
        pl.when(at > 0)(down.wait_send)

    def start_yz(self, step):
        self.z_copy(step).start()
        self.start(self.y_copies(step))

    def start_all(self, step):
        self.start(self.x_copies(step))
        self.start_yz(step)

    def wait_yz(self, step):
        self.wait_recv(self.y_copies(step))
        self.z_copy(step).wait_recv()

    def wait_x(self, step):
        self.wait_recv(self.x_copies(step))

    def wait_sends(self, step):
        self.wait_send(self.x_copies(step))
        self.wait_send(self.y_copies(step))
        self.z_copy(step).wait_send()

    def pack(self, step, x, value):
        ny, lanes = self.ny, self.lanes
        self.y_send[step, 0, pl.ds(x, 1), :] = value[0:1]
        self.y_send[step, 1, pl.ds(x, 1), :] = value[ny - 1:ny]
        if lanes > LANES:
            tile = jnp.where(self.gz == 0, value[:, lanes - LANES:], value[:, :LANES])
        else:
            tile = value
        edge = lax.rem(self.edge, LANES)
        turned = pltpu.roll(tile, lax.rem(x - edge + LANES, LANES), 1)
        lane = lax.broadcasted_iota(jnp.int32, (ny, LANES), 1)
        self.z_send[step] = jnp.where(lane == x, turned, self.z_send[step])

    def around(self, step, x):
        ny, lanes = self.ny, self.lanes
        field = self.fields.at[step]
        value = field[x + 1]
        total = field[x] + field[x + 2]
        row = lax.broadcasted_iota(jnp.int32, (ny, lanes), 0)
        lane = lax.broadcasted_iota(jnp.int32, (ny, lanes), 1)
        below = self.y_recv[step, 0, pl.ds(x, 1), :]
        above = self.y_recv[step, 1, pl.ds(x, 1), :]
        total = total + jnp.where(row == 0, below, pltpu.roll(value, 1, 0))
        total = total + jnp.where(row == ny - 1, above, pltpu.roll(value, ny - 1, 0))
        total = total + jnp.where(lane == 0, 0.0, pltpu.roll(value, 1, 1))
        total = total + jnp.where(lane == lanes - 1, 0.0, pltpu.roll(value, lanes - 1, 1))
        edge = lax.rem(self.edge, LANES)
        face = pltpu.roll(self.z_recv[step], lax.rem(edge - x + LANES, LANES), 1)
        if lanes > LANES:
            face = jnp.concatenate([face] * (lanes // LANES), axis=1)
        return value, total + jnp.where(lane == self.edge, face, 0.0)


def kernel(counts, rhs_hbm, guess_hbm, damp_hbm, group_hbm, inverse_hbm,
           fine_hbm, middle_hbm, coarse_hbm, solved_ref,
           f_fields, f_ys, f_yr, f_zs, f_zr,
           m_fields, m_ys, m_yr, m_zs, m_zr,
           c_fields, c_ys, c_yr, c_zs, c_zr,
           rhs, damp, group, inverse, weight, scaled,
           m_damp, m_src, m_weight, m_scaled, c_damp, c_src, c_weight, c_scaled,
           halves, quarters, c_defect, c_out, group_rows, onehot, reduced, gathered,
           f_send, f_recv, m_send, m_recv, c_send, c_recv,
           r_send, r_recv, g_send, g_recv, local_sem):
    place = gx, gy, gz = lax.axis_index("gx"), lax.axis_index("gy"), lax.axis_index("gz")
    cx, cy, cz = counts
    bx, by, bz = rhs.shape
    fine = Level((bx, by, bz), bz, f_fields, f_ys, f_yr, f_zs, f_zr, (f_send, f_recv), place, counts)
    middle = Level((bx // 2, by // 2, bz // 2), bz // 2, m_fields, m_ys, m_yr, m_zs, m_zr,
                   (m_send, m_recv), place, counts)
    coarse = Level((bx // 4, by // 4, bz // 4), LANES, c_fields, c_ys, c_yr, c_zs, c_zr,
                   (c_send, c_recv), place, counts)

    loads = [
        pltpu.make_async_copy(guess_hbm, f_fields.at[0, pl.ds(1, bx)], local_sem.at[0]),
        pltpu.make_async_copy(damp_hbm, damp, local_sem.at[1]),
        pltpu.make_async_copy(rhs_hbm, rhs, local_sem.at[2]),
        pltpu.make_async_copy(group_hbm, group, local_sem.at[3]),
        pltpu.make_async_copy(inverse_hbm, inverse, local_sem.at[4]),
    ]
    for load in loads:
        load.start()

    mates = [(i, k) for i in range(cx) for k in range(cz)]
    barrier = pltpu.get_barrier_semaphore()
    for i, k in mates:
        @pl.when(jnp.logical_or(gx != i, gz != k))
        def _():
            pl.semaphore_signal(barrier, inc=1, device_id=(i, gy, k), device_id_type=MESH)
    for j in range(cy):
        @pl.when(gy != j)
        def _():
            pl.semaphore_signal(barrier, inc=1, device_id=(gx, j, gz), device_id_type=MESH)

    for level in (fine, middle, coarse):
        level.clear()
    pl.semaphore_wait(barrier, len(mates) - 1 + cy - 1)

    first_x = fine.x_copies(0, guess_hbm.at[0], guess_hbm.at[bx - 1])
    fine.start(first_x)
    loads[0].wait()

    @pl.loop(0, bx)
    def _(x):
        fine.pack(0, x, f_fields[0, x + 1])

    fine.start_yz(0)

    loads[1].wait()
    loads[2].wait()
    pair_fine = pair_matrix(bz, bz // 2)
    pair_middle = pair_matrix(bz // 2, LANES)

    @pl.loop(0, bx)
    def _(x):
        factor = OMEGA / (6.0 + damp[x])
        weight[x] = factor
        scaled[x] = factor * rhs[x]

    def shrink_to(source, target, scratch, pairs, nx, ny):
        for x in range(nx):
            both = source(2 * x) + source(2 * x + 1)
            scratch[pl.ds(x * 2 * ny, 2 * ny), :] = split_dot(both, pairs, (((1,), (0,)), ((), ())))
        for x in range(nx):
            even = scratch[pl.ds(x * 2 * ny, ny, stride=2), :]
            odd = scratch[pl.ds(x * 2 * ny + 1, ny, stride=2), :]
            target[x] = 0.5 * (even + odd)

    shrink_to(lambda x: damp[x], m_damp, halves, pair_fine, middle.nx, middle.ny)
    shrink_to(lambda x: m_damp[x], c_damp, quarters, pair_middle, coarse.nx, coarse.ny)
    c_lane = lax.broadcasted_iota(jnp.int32, (coarse.nx, coarse.ny, LANES), 2)
    m_weight[...] = OMEGA / (6.0 + m_damp[...])
    c_weight[...] = jnp.where(c_lane < coarse.nz, OMEGA / (6.0 + c_damp[...]), 0.0)

    loads[3].wait()
    rows = coarse.nx * coarse.ny
    cells = coarse.nz
    group_rows[...] = jnp.zeros((rows, LANES), jnp.int32)
    for x in range(coarse.nx):
        group_rows[pl.ds(x * coarse.ny, coarse.ny), pl.ds(0, cells)] = group[x]
    packed = group_rows[pl.ds(0, rows // 2), :]
    packed = packed + pltpu.roll(group_rows[pl.ds(rows // 2, rows // 2), :], cells, 1)
    group_rows[pl.ds(0, rows // 2), :] = packed
    half = rows // 4

    @pl.loop(0, half)
    def _(row):
        number = lax.broadcasted_iota(jnp.int32, (LANES, LANES), 0)
        for part in range(2):
            low = group_rows[pl.ds(row + part * half, 1), :] & (LANES - 1)
            onehot[row, :, part * LANES:(part + 1) * LANES] = jnp.where(
                number == low, 1.0, 0.0).astype(jnp.bfloat16)

    def sweep(level, step, weights, scaleds, planes, unroll=1):
        def one(x):
            value, total = level.around(step, x)
            new = (1.0 - OMEGA) * value + (scaleds[x] + weights[x] * total)
            level.fields[step + 1, x + 1] = new
            level.pack(step + 1, x, new)

        level.wait_yz(step)

        @pl.loop(1, planes - 1)
        def _(x):
            one(x)

        level.wait_x(step)
        one(0)
        one(planes - 1)
        level.start_all(step + 1)

    for step in range(SWEEPS):
        sweep(fine, step, weight, scaled, bx)
    store_fine = pltpu.make_async_copy(f_fields.at[SWEEPS, pl.ds(1, bx)], fine_hbm, local_sem.at[5])
    store_fine.start()

    fine.wait_yz(SWEEPS)

    def defect_pair(x):
        total = None
        for plane in (2 * x, 2 * x + 1):
            value, around = fine.around(SWEEPS, plane)
            part = rhs[plane] - ((6.0 + damp[plane]) * value - around)
            total = part if total is None else total + part
        halves[pl.ds(pl.multiple_of(x * by, by), by), :] = split_dot(total, pair_fine, (((1,), (0,)), ((), ())))

    @pl.loop(1, middle.nx - 1)
    def _(x):
        defect_pair(x)

    fine.wait_x(SWEEPS)
    defect_pair(0)
    defect_pair(middle.nx - 1)

    def enter(level, scratch, source, weights, scaleds):
        ny = level.ny
        for x in range(level.nx):
            even = scratch[pl.ds(x * 2 * ny, ny, stride=2), :]
            odd = scratch[pl.ds(x * 2 * ny + 1, ny, stride=2), :]
            source[x] = 0.5 * (even + odd)
            scaleds[x] = weights[x] * source[x]
            level.fields[0, x + 1] = scaleds[x]
            level.pack(0, x, scaleds[x])
        level.start_all(0)

    enter(middle, halves, m_src, m_weight, m_scaled)
    for step in range(SWEEPS - 1):
        sweep(middle, step, m_weight, m_scaled, middle.nx)
    last = SWEEPS - 1
    store_middle = pltpu.make_async_copy(m_fields.at[last, pl.ds(1, middle.nx)], middle_hbm, local_sem.at[6])
    store_middle.start()
    middle.wait_yz(last)
    middle.wait_x(last)

    my = middle.ny
    for x in range(coarse.nx):
        total = None
        for plane in (2 * x, 2 * x + 1):
            value, around = middle.around(last, plane)
            part = m_src[plane] - ((6.0 + m_damp[plane]) * value - around)
            total = part if total is None else total + part
        quarters[pl.ds(x * my, my), :] = split_dot(total, pair_middle, (((1,), (0,)), ((), ())))

    enter(coarse, quarters, c_src, c_weight, c_scaled)
    for step in range(SWEEPS - 1):
        sweep(coarse, step, c_weight, c_scaled, coarse.nx)
    for x in range(coarse.nx):
        c_out[x] = c_fields[last, x + 1][:, :cells]
    store_coarse = pltpu.make_async_copy(c_out, coarse_hbm, local_sem.at[7])
    store_coarse.start()
    coarse.wait_yz(last)
    coarse.wait_x(last)
    valid = lax.broadcasted_iota(jnp.int32, (coarse.ny, LANES), 1) < cells
    for x in range(coarse.nx):
        value, around = coarse.around(last, x)
        part = c_src[x] - ((6.0 + c_damp[x]) * value - around)
        c_defect[pl.ds(x * coarse.ny, coarse.ny), :] = jnp.where(valid, part, 0.0)

    packed = c_defect[pl.ds(0, rows // 2), :]
    packed = packed + pltpu.roll(c_defect[pl.ds(rows // 2, rows // 2), :], cells, 1)
    c_defect[pl.ds(0, rows // 2), :] = packed

    tall = NAGG // LANES

    def gather_row(row, total):
        number = lax.broadcasted_iota(jnp.int32, (tall, LANES), 0)
        parts = []
        for part in range(2):
            at = pl.ds(row + part * half, 1)
            high = group_rows[at, :] // LANES
            parts.append(jnp.where(number == high, c_defect[at, :], 0.0))
        values = jnp.concatenate(parts, axis=1)
        first = values.astype(jnp.bfloat16).astype(jnp.float32)
        both = jnp.concatenate([first, values - first], axis=0).astype(jnp.bfloat16)
        return total + lax.dot_general(both, onehot[row], (((1,), (1,)), ((), ())),
                                       preferred_element_type=jnp.float32)

    sums = lax.fori_loop(0, half, gather_row, jnp.zeros((2 * tall, LANES), jnp.float32))
    mine = gx * cz + gz
    reduced[mine] = sums[:tall] + sums[tall:]

    def reduce_copy(i, k):
        return pltpu.make_async_remote_copy(
            src_ref=reduced.at[mine], dst_ref=reduced.at[mine],
            send_sem=r_send.at[i * cz + k], recv_sem=r_recv.at[mine],
            device_id=(i, gy, k), device_id_type=MESH)

    def reduce_wait(i, k):
        return pltpu.make_async_remote_copy(
            src_ref=reduced.at[i * cz + k], dst_ref=reduced.at[i * cz + k],
            send_sem=r_send.at[i * cz + k], recv_sem=r_recv.at[i * cz + k],
            device_id=(i, gy, k), device_id_type=MESH)

    def mates_do(act):
        for i, k in mates:
            pl.when(jnp.logical_or(gx != i, gz != k))(functools.partial(act, i, k))

    mates_do(lambda i, k: reduce_copy(i, k).start())
    mates_do(lambda i, k: reduce_wait(i, k).wait_recv())
    gathered[gy] = jnp.sum(reduced[...], axis=0)

    def gather_copy(j, slot, recv):
        return pltpu.make_async_remote_copy(
            src_ref=gathered.at[slot], dst_ref=gathered.at[slot],
            send_sem=g_send.at[j], recv_sem=g_recv.at[recv],
            device_id=(gx, j, gz), device_id_type=MESH)

    for j in range(cy):
        pl.when(gy != j)(lambda j=j: gather_copy(j, gy, gy).start())
    for j in range(cy):
        pl.when(gy != j)(lambda j=j: gather_copy(j, j, j).wait_recv())
    total_cells = rows * cells * cx * cy * cz
    source = jnp.sum(gathered[...], axis=0) * (1.0 / math.sqrt(total_cells // NAGG))

    loads[4].wait()
    out_rows = inverse.shape[0]
    product = None
    for part in range(tall):
        term = inverse[:, part * LANES:(part + 1) * LANES] * source[part:part + 1]
        product = term if product is None else product + term
    ones = jnp.ones((8, LANES), jnp.float32)
    solved = lax.dot_general(ones, product, (((1,), (1,)), ((), ())),
                             precision=lax.Precision.HIGHEST, preferred_element_type=jnp.float32)
    solved_ref[...] = solved[0:1]

    for step in range(SWEEPS + 1):
        if step == 0:
            fine.wait_send(first_x)
            fine.wait_send(fine.y_copies(0))
            fine.z_copy(0).wait_send()
        else:
            fine.wait_sends(step)
    for step in range(SWEEPS):
        middle.wait_sends(step)
        coarse.wait_sends(step)
    mates_do(lambda i, k: reduce_copy(i, k).wait_send())
    for j in range(cy):
        pl.when(gy != j)(lambda j=j: gather_copy(j, gy, gy).wait_send())
    store_fine.wait()
    store_middle.wait()
    store_coarse.wait()


def shards(counts, right_side, initial_guess, damping, group_map, block_inverse):
    bx, by, bz = right_side.shape
    f32 = jnp.float32
    vm = pltpu.VMEM

    def level_scratch(nx, ny, lanes, rounds):
        return [
            vm((rounds, nx + 2, ny, lanes), f32),
            vm((rounds, 2, nx, lanes), f32), vm((rounds, 2, nx, lanes), f32),
            vm((rounds, ny, LANES), f32), vm((rounds, ny, LANES), f32),
        ]

    cx, cy, cz = counts
    mid = (bx // 2, by // 2, bz // 2)
    low = (bx // 4, by // 4, bz // 4)
    low_pad = (low[0], low[1], LANES)
    rows = low[0] * low[1]
    out_rows = block_inverse.shape[0]
    dma = pltpu.SemaphoreType.DMA
    any_space = pl.BlockSpec(memory_space=pl.ANY)
    outs = pl.pallas_call(
        functools.partial(kernel, counts),
        out_shape=(
            jax.ShapeDtypeStruct((bx, by, bz), f32),
            jax.ShapeDtypeStruct(mid, f32),
            jax.ShapeDtypeStruct(low, f32),
            jax.ShapeDtypeStruct((1, out_rows), f32),
        ),
        in_specs=[any_space] * 5,
        out_specs=(any_space, any_space, any_space, pl.BlockSpec(memory_space=pltpu.VMEM)),
        scratch_shapes=[
            *level_scratch(bx, by, bz, SWEEPS + 1),
            *level_scratch(*mid, SWEEPS),
            *level_scratch(*low_pad, SWEEPS),
            vm((bx, by, bz), f32), vm((bx, by, bz), f32), vm(low, jnp.int32), vm(block_inverse.shape, f32),
            vm((bx, by, bz), f32), vm((bx, by, bz), f32),
            vm(mid, f32), vm(mid, f32), vm(mid, f32), vm(mid, f32),
            vm(low_pad, f32), vm(low_pad, f32), vm(low_pad, f32), vm(low_pad, f32),
            vm((mid[0] * by, LANES), f32), vm((low[0] * mid[1], LANES), f32),
            vm((rows, LANES), f32), vm(low, f32), vm((rows, LANES), jnp.int32),
            vm((rows // 4, LANES, 2 * LANES), jnp.bfloat16),
            vm((cx * cz, NAGG // LANES, LANES), f32), vm((cy, NAGG // LANES, LANES), f32),
            dma((SWEEPS + 1, 5)), dma((SWEEPS + 1, 5)),
            dma((SWEEPS, 5)), dma((SWEEPS, 5)), dma((SWEEPS, 5)), dma((SWEEPS, 5)),
            dma((cx * cz,)), dma((cx * cz,)), dma((cy,)), dma((cy,)), dma((8,)),
        ],
        compiler_params=pltpu.CompilerParams(
            collective_id=0, has_side_effects=True, vmem_limit_bytes=48 * 1024 * 1024),
        cost_estimate=pl.CostEstimate(flops=40_000_000, bytes_accessed=6_000_000, transcendentals=0),
    )(right_side, initial_guess, damping, group_map, block_inverse)
    fine, middle, coarse, solved = outs
    return fine, middle, coarse, solved.reshape(out_rows)


def solution(mesh):
    counts = tuple(mesh.shape[axis] for axis in ("gx", "gy", "gz"))
    cells = P("gx", "gy", "gz")
    return jax.shard_map(
        functools.partial(shards, counts),
        mesh=mesh,
        in_specs=(cells, cells, cells, cells, P("gy", None)),
        out_specs=(cells, cells, cells, P("gy")),
        check_vma=False,
    )
```

```python
import functools
import math

import jax
import jax.numpy as jnp
from jax import lax
from jax.experimental import pallas as pl
from jax.experimental.pallas import tpu as pltpu
from jax.sharding import PartitionSpec as P

SWEEPS = 4
NAGG = 1024
OMEGA = 0.8
LANES = 128
MESH = pl.DeviceIdType.MESH


def split_dot(left, right_bf16, dims):
    high = left.astype(jnp.bfloat16)
    low = (left - high.astype(jnp.float32)).astype(jnp.bfloat16)
    out = lax.dot_general(high, right_bf16, dims, preferred_element_type=jnp.float32)
    return out + lax.dot_general(low, right_bf16, dims, preferred_element_type=jnp.float32)


def pair_matrix(rows, columns):
    row = lax.broadcasted_iota(jnp.int32, (rows, columns), 0)
    column = lax.broadcasted_iota(jnp.int32, (rows, columns), 1)
    first = jnp.where(row == 2 * column, 1.0, 0.0)
    return (first + jnp.where(row == 2 * column + 1, 1.0, 0.0)).astype(jnp.bfloat16)


class Level:
    def __init__(self, dims, lanes, fields, y_send, y_recv, z_send, z_recv, sems, place, counts):
        self.nx, self.ny, self.nz = dims
        self.lanes = lanes
        self.fields, self.y_send, self.y_recv = fields, y_send, y_recv
        self.z_send, self.z_recv = z_send, z_recv
        self.send_sem, self.recv_sem = sems
        self.gx, self.gy, self.gz = place
        self.counts = counts
        self.edge = jnp.where(self.gz == 0, self.nz - 1, 0)

    def clear(self):
        nx, ny, lanes = self.nx, self.ny, self.lanes
        rounds = len(self.fields)

        @pl.when(self.gx == 0)
        def _():
            for step in range(rounds):
                self.fields[step][0] = jnp.zeros((ny, lanes), jnp.float32)

        @pl.when(self.gx == self.counts[0] - 1)
        def _():
            for step in range(rounds):
                self.fields[step][nx + 1] = jnp.zeros((ny, lanes), jnp.float32)

        @pl.when(self.gy == 0)
        def _():
            for step in range(rounds):
                self.y_recv[step, 0] = jnp.zeros((nx, lanes), jnp.float32)

        @pl.when(self.gy == self.counts[1] - 1)
        def _():
            for step in range(rounds):
                self.y_recv[step, 1] = jnp.zeros((nx, lanes), jnp.float32)

        for step in range(rounds):
            self.z_send[step] = jnp.zeros((ny, LANES), jnp.float32)

    def x_copies(self, step, low=None, high=None):
        gx, gy, gz = self.gx, self.gy, self.gz
        field = self.fields[step]
        low = field.at[1] if low is None else low
        high = field.at[self.nx] if high is None else high
        up = pltpu.make_async_remote_copy(
            src_ref=high, dst_ref=field.at[0],
            send_sem=self.send_sem.at[step, 0], recv_sem=self.recv_sem.at[step, 0],
            device_id=(gx + 1, gy, gz), device_id_type=MESH)
        down = pltpu.make_async_remote_copy(
            src_ref=low, dst_ref=field.at[self.nx + 1],
            send_sem=self.send_sem.at[step, 1], recv_sem=self.recv_sem.at[step, 1],
            device_id=(gx - 1, gy, gz), device_id_type=MESH)
        return (gx, self.counts[0], up, down)

    def y_copies(self, step):
        gx, gy, gz = self.gx, self.gy, self.gz
        up = pltpu.make_async_remote_copy(
            src_ref=self.y_send.at[step, 1], dst_ref=self.y_recv.at[step, 0],
            send_sem=self.send_sem.at[step, 2], recv_sem=self.recv_sem.at[step, 2],
            device_id=(gx, gy + 1, gz), device_id_type=MESH)
        down = pltpu.make_async_remote_copy(
            src_ref=self.y_send.at[step, 0], dst_ref=self.y_recv.at[step, 1],
            send_sem=self.send_sem.at[step, 3], recv_sem=self.recv_sem.at[step, 3],
            device_id=(gx, gy - 1, gz), device_id_type=MESH)
        return (gy, self.counts[1], up, down)

    def z_copy(self, step):
        return pltpu.make_async_remote_copy(
            src_ref=self.z_send.at[step], dst_ref=self.z_recv.at[step],
            send_sem=self.send_sem.at[step, 4], recv_sem=self.recv_sem.at[step, 4],
            device_id=(self.gx, self.gy, 1 - self.gz), device_id_type=MESH)

    @staticmethod
    def start(copies):
        at, count, up, down = copies
        pl.when(at < count - 1)(up.start)
        pl.when(at > 0)(down.start)

    @staticmethod
    def wait_recv(copies):
        at, count, up, down = copies
        pl.when(at > 0)(up.wait_recv)
        pl.when(at < count - 1)(down.wait_recv)

    @staticmethod
    def wait_send(copies):
        at, count, up, down = copies
        pl.when(at < count - 1)(up.wait_send)
        pl.when(at > 0)(down.wait_send)

    def start_yz(self, step):
        self.z_copy(step).start()
        self.start(self.y_copies(step))

    def start_all(self, step):
        self.start(self.x_copies(step))
        self.start_yz(step)

    def wait_yz(self, step):
        self.wait_recv(self.y_copies(step))
        self.z_copy(step).wait_recv()

    def wait_x(self, step):
        self.wait_recv(self.x_copies(step))

    def wait_sends(self, step):
        self.wait_send(self.x_copies(step))
        self.wait_send(self.y_copies(step))
        self.z_copy(step).wait_send()

    def pack(self, step, x, value, face):
        ny, lanes = self.ny, self.lanes
        self.y_send[step, 0, pl.ds(x, 1), :] = value[0:1]
        self.y_send[step, 1, pl.ds(x, 1), :] = value[ny - 1:ny]
        if lanes > LANES:
            tile = jnp.where(self.gz == 0, value[:, lanes - LANES:], value[:, :LANES])
        else:
            tile = value
        edge = lax.rem(self.edge, LANES)
        turned = pltpu.roll(tile, lax.rem(x - edge + LANES, LANES), 1)
        lane = lax.broadcasted_iota(jnp.int32, (ny, LANES), 1)
        return jnp.where(lane == x, turned, face)

    def around(self, step, x):
        ny, lanes = self.ny, self.lanes
        field = self.fields[step]
        value = field[x + 1]
        below = self.y_recv[step, 0, pl.ds(x, 1), :]
        above = self.y_recv[step, 1, pl.ds(x, 1), :]
        total = field[x] + field[x + 2]
        total = total + jnp.concatenate([below, value[:ny - 1]], axis=0)
        total = total + jnp.concatenate([value[1:], above], axis=0)
        lane = lax.broadcasted_iota(jnp.int32, (ny, LANES), 1)
        face = pltpu.roll(self.z_recv[step], lax.rem(lax.rem(self.edge, LANES) - x + LANES, LANES), 1)
        left_face = jnp.where(self.gz == 0, 0.0, face)
        right_face = jnp.where(self.gz == 0, face, 0.0)
        tiles = [value[:, at:at + LANES] for at in range(0, lanes, LANES)]
        lefts = [left_face] + [pltpu.roll(tile, 1, 1) for tile in tiles]
        rights = [pltpu.roll(tile, LANES - 1, 1) for tile in tiles] + [right_face]
        sides = []
        for at in range(len(tiles)):
            right = rights[at]
            if at + 1 < len(tiles) or self.nz == lanes:
                right = jnp.where(lane == LANES - 1, rights[at + 1], right)
            else:
                right = jnp.where(lane == self.nz - 1, right_face, right)
            sides.append(jnp.where(lane == 0, lefts[at], lefts[at + 1]) + right)
        around = sides[0] if len(sides) == 1 else jnp.concatenate(sides, axis=1)
        return value, total + around


def kernel(counts, rhs_hbm, guess_hbm, damp_hbm, group_hbm, inverse_hbm,
           fine_hbm, middle_hbm, coarse_hbm, solved_ref,
           f_fields, f_ys, f_yr, f_zs, f_zr,
           m_fields, m_ys, m_yr, m_zs, m_zr,
           c_fields, c_ys, c_yr, c_zs, c_zr,
           rhs, damp, group, inverse, weight, scaled,
           m_damp, m_src, m_weight, m_scaled, c_damp, c_src, c_weight, c_scaled,
           halves, quarters, c_defect, c_out, group_rows, onehot, reduced, gathered,
           f_send, f_recv, m_send, m_recv, c_send, c_recv,
           r_send, r_recv, g_send, g_recv, local_sem):
    place = gx, gy, gz = lax.axis_index("gx"), lax.axis_index("gy"), lax.axis_index("gz")
    cx, cy, cz = counts
    bx, by, bz = rhs.shape
    fine = Level((bx, by, bz), bz, f_fields, f_ys, f_yr, f_zs, f_zr, (f_send, f_recv), place, counts)
    middle = Level((bx // 2, by // 2, bz // 2), bz // 2, m_fields, m_ys, m_yr, m_zs, m_zr,
                   (m_send, m_recv), place, counts)
    coarse = Level((bx // 4, by // 4, bz // 4), LANES, c_fields, c_ys, c_yr, c_zs, c_zr,
                   (c_send, c_recv), place, counts)

    loads = [
        pltpu.make_async_copy(guess_hbm, f_fields[0].at[pl.ds(1, bx)], local_sem.at[0]),
        pltpu.make_async_copy(damp_hbm, damp, local_sem.at[1]),
        pltpu.make_async_copy(rhs_hbm, rhs, local_sem.at[2]),
        pltpu.make_async_copy(group_hbm, group, local_sem.at[3]),
        pltpu.make_async_copy(inverse_hbm, inverse, local_sem.at[4]),
    ]
    for load in loads:
        load.start()

    mates = [(i, k) for i in range(cx) for k in range(cz)]
    barrier = pltpu.get_barrier_semaphore()
    for i, k in mates:
        @pl.when(jnp.logical_or(gx != i, gz != k))
        def _():
            pl.semaphore_signal(barrier, inc=1, device_id=(i, gy, k), device_id_type=MESH)
    for j in range(cy):
        @pl.when(gy != j)
        def _():
            pl.semaphore_signal(barrier, inc=1, device_id=(gx, j, gz), device_id_type=MESH)

    for level in (fine, middle, coarse):
        level.clear()
    pl.semaphore_wait(barrier, len(mates) - 1 + cy - 1)

    first_x = fine.x_copies(0, guess_hbm.at[0], guess_hbm.at[bx - 1])
    fine.start(first_x)
    loads[0].wait()

    @pl.loop(0, bx // 4)
    def _(group):
        face = f_zs[0]
        for part in range(4):
            x = group * 4 + part
            face = fine.pack(0, x, f_fields[0][x + 1], face)
        f_zs[0] = face

    fine.start_yz(0)

    loads[1].wait()
    loads[2].wait()
    pair_fine = pair_matrix(bz, bz // 2)
    pair_middle = pair_matrix(bz // 2, LANES)

    @pl.loop(0, bx, unroll=4)
    def _(x):
        factor = OMEGA / (6.0 + damp[x])
        weight[x] = factor
        scaled[x] = factor * rhs[x]

    def shrink_to(source, target, scratch, pairs, nx, ny):
        for x in range(nx):
            both = source(2 * x) + source(2 * x + 1)
            scratch[pl.ds(x * 2 * ny, 2 * ny), :] = split_dot(both, pairs, (((1,), (0,)), ((), ())))
        for x in range(nx):
            even = scratch[pl.ds(x * 2 * ny, ny, stride=2), :]
            odd = scratch[pl.ds(x * 2 * ny + 1, ny, stride=2), :]
            target[x] = 0.5 * (even + odd)

    shrink_to(lambda x: damp[x], m_damp, halves, pair_fine, middle.nx, middle.ny)
    shrink_to(lambda x: m_damp[x], c_damp, quarters, pair_middle, coarse.nx, coarse.ny)
    c_lane = lax.broadcasted_iota(jnp.int32, (coarse.nx, coarse.ny, LANES), 2)
    m_weight[...] = OMEGA / (6.0 + m_damp[...])
    c_weight[...] = jnp.where(c_lane < coarse.nz, OMEGA / (6.0 + c_damp[...]), 0.0)

    loads[3].wait()
    rows = coarse.nx * coarse.ny
    cells = coarse.nz
    group_rows[...] = jnp.zeros((rows, LANES), jnp.int32)
    for x in range(coarse.nx):
        group_rows[pl.ds(x * coarse.ny, coarse.ny), pl.ds(0, cells)] = group[x]
    packed = group_rows[pl.ds(0, rows // 2), :]
    packed = packed + pltpu.roll(group_rows[pl.ds(rows // 2, rows // 2), :], cells, 1)
    group_rows[pl.ds(0, rows // 2), :] = packed
    half = rows // 4

    @pl.loop(0, half, unroll=4)
    def _(row):
        number = lax.broadcasted_iota(jnp.int32, (LANES, LANES), 0)
        for part in range(2):
            low = group_rows[pl.ds(row + part * half, 1), :] & (LANES - 1)
            onehot[row, :, part * LANES:(part + 1) * LANES] = jnp.where(
                number == low, 1.0, 0.0).astype(jnp.bfloat16)

    def sweep(level, step, weights, scaleds, planes):
        def one(x, face):
            value, total = level.around(step, x)
            new = (1.0 - OMEGA) * value + (scaleds[x] + weights[x] * total)
            level.fields[step + 1][x + 1] = new
            return level.pack(step + 1, x, new, face)

        level.wait_yz(step)
        size = 2 if planes > 8 else planes - 2

        def some(first):
            face = level.z_send[step + 1]
            for part in range(size):
                face = one(first + part, face)
            level.z_send[step + 1] = face

        if size == planes - 2:
            some(1)
        else:
            @pl.loop(0, (planes - 2) // size)
            def _(group):
                some(group * size + 1)

        level.wait_x(step)
        face = one(0, level.z_send[step + 1])
        face = one(planes - 1, face)
        level.start(level.x_copies(step + 1))
        level.z_send[step + 1] = face
        level.start_yz(step + 1)

    for step in range(SWEEPS):
        sweep(fine, step, weight, scaled, bx)
    store_fine = pltpu.make_async_copy(f_fields[SWEEPS].at[pl.ds(1, bx)], fine_hbm, local_sem.at[5])
    store_fine.start()

    fine.wait_yz(SWEEPS)

    def defect_pair(x):
        total = None
        for plane in (2 * x, 2 * x + 1):
            value, around = fine.around(SWEEPS, plane)
            part = rhs[plane] - ((6.0 + damp[plane]) * value - around)
            total = part if total is None else total + part
        halves[pl.ds(pl.multiple_of(x * by, by), by), :] = split_dot(total, pair_fine, (((1,), (0,)), ((), ())))

    @pl.loop(1, middle.nx - 1, unroll=2)
    def _(x):
        defect_pair(x)

    fine.wait_x(SWEEPS)
    defect_pair(0)
    defect_pair(middle.nx - 1)

    def enter(level, scratch, source, weights, scaleds):
        ny = level.ny
        face = jnp.zeros((ny, LANES), jnp.float32)
        for x in range(level.nx):
            even = scratch[pl.ds(x * 2 * ny, ny, stride=2), :]
            odd = scratch[pl.ds(x * 2 * ny + 1, ny, stride=2), :]
            source[x] = 0.5 * (even + odd)
            new = weights[x] * source[x]
            scaleds[x] = new
            level.fields[0][x + 1] = new
            face = level.pack(0, x, new, face)
        level.z_send[0] = face
        level.start_all(0)

    enter(middle, halves, m_src, m_weight, m_scaled)
    for step in range(SWEEPS - 1):
        sweep(middle, step, m_weight, m_scaled, middle.nx)
    last = SWEEPS - 1
    store_middle = pltpu.make_async_copy(m_fields[last].at[pl.ds(1, middle.nx)], middle_hbm, local_sem.at[6])
    store_middle.start()
    middle.wait_yz(last)
    middle.wait_x(last)

    my = middle.ny
    for x in range(coarse.nx):
        total = None
        for plane in (2 * x, 2 * x + 1):
            value, around = middle.around(last, plane)
            part = m_src[plane] - ((6.0 + m_damp[plane]) * value - around)
            total = part if total is None else total + part
        quarters[pl.ds(x * my, my), :] = split_dot(total, pair_middle, (((1,), (0,)), ((), ())))

    enter(coarse, quarters, c_src, c_weight, c_scaled)
    for step in range(SWEEPS - 1):
        sweep(coarse, step, c_weight, c_scaled, coarse.nx)
    for x in range(coarse.nx):
        c_out[x] = c_fields[last][x + 1][:, :cells]
    store_coarse = pltpu.make_async_copy(c_out, coarse_hbm, local_sem.at[7])
    store_coarse.start()
    coarse.wait_yz(last)
    coarse.wait_x(last)
    valid = lax.broadcasted_iota(jnp.int32, (coarse.ny, LANES), 1) < cells
    for x in range(coarse.nx):
        value, around = coarse.around(last, x)
        part = c_src[x] - ((6.0 + c_damp[x]) * value - around)
        c_defect[pl.ds(x * coarse.ny, coarse.ny), :] = jnp.where(valid, part, 0.0)

    packed = c_defect[pl.ds(0, rows // 2), :]
    packed = packed + pltpu.roll(c_defect[pl.ds(rows // 2, rows // 2), :], cells, 1)
    c_defect[pl.ds(0, rows // 2), :] = packed

    tall = NAGG // LANES

    def gather_row(row, total):
        number = lax.broadcasted_iota(jnp.int32, (tall, LANES), 0)
        parts = []
        for part in range(2):
            at = pl.ds(row + part * half, 1)
            high = group_rows[at, :] // LANES
            parts.append(jnp.where(number == high, c_defect[at, :], 0.0))
        values = jnp.concatenate(parts, axis=1)
        first = values.astype(jnp.bfloat16).astype(jnp.float32)
        both = jnp.concatenate([first, values - first], axis=0).astype(jnp.bfloat16)
        return total + lax.dot_general(both, onehot[row], (((1,), (1,)), ((), ())),
                                       preferred_element_type=jnp.float32)

    sums = lax.fori_loop(0, half, gather_row, jnp.zeros((2 * tall, LANES), jnp.float32),
                         unroll=4)
    mine = gx * cz + gz
    reduced[mine] = sums[:tall] + sums[tall:]

    def reduce_copy(i, k):
        return pltpu.make_async_remote_copy(
            src_ref=reduced.at[mine], dst_ref=reduced.at[mine],
            send_sem=r_send.at[i * cz + k], recv_sem=r_recv.at[mine],
            device_id=(i, gy, k), device_id_type=MESH)

    def reduce_wait(i, k):
        return pltpu.make_async_remote_copy(
            src_ref=reduced.at[i * cz + k], dst_ref=reduced.at[i * cz + k],
            send_sem=r_send.at[i * cz + k], recv_sem=r_recv.at[i * cz + k],
            device_id=(i, gy, k), device_id_type=MESH)

    def mates_do(act):
        for i, k in mates:
            pl.when(jnp.logical_or(gx != i, gz != k))(functools.partial(act, i, k))

    mates_do(lambda i, k: reduce_copy(i, k).start())
    mates_do(lambda i, k: reduce_wait(i, k).wait_recv())
    gathered[gy] = jnp.sum(reduced[...], axis=0)

    def gather_copy(j, slot, recv):
        return pltpu.make_async_remote_copy(
            src_ref=gathered.at[slot], dst_ref=gathered.at[slot],
            send_sem=g_send.at[j], recv_sem=g_recv.at[recv],
            device_id=(gx, j, gz), device_id_type=MESH)

    for j in range(cy):
        pl.when(gy != j)(lambda j=j: gather_copy(j, gy, gy).start())
    for j in range(cy):
        pl.when(gy != j)(lambda j=j: gather_copy(j, j, j).wait_recv())
    total_cells = rows * cells * cx * cy * cz
    source = jnp.sum(gathered[...], axis=0) * (1.0 / math.sqrt(total_cells // NAGG))

    loads[4].wait()
    out_rows = inverse.shape[0]
    product = None
    for part in range(tall):
        term = inverse[:, part * LANES:(part + 1) * LANES] * source[part:part + 1]
        product = term if product is None else product + term
    ones = jnp.ones((8, LANES), jnp.float32)
    solved = lax.dot_general(ones, product, (((1,), (1,)), ((), ())),
                             precision=lax.Precision.HIGHEST, preferred_element_type=jnp.float32)
    solved_ref[...] = solved[0:1]

    for step in range(SWEEPS + 1):
        if step == 0:
            fine.wait_send(first_x)
            fine.wait_send(fine.y_copies(0))
            fine.z_copy(0).wait_send()
        else:
            fine.wait_sends(step)
    for step in range(SWEEPS):
        middle.wait_sends(step)
        coarse.wait_sends(step)
    mates_do(lambda i, k: reduce_copy(i, k).wait_send())
    for j in range(cy):
        pl.when(gy != j)(lambda j=j: gather_copy(j, gy, gy).wait_send())
    store_fine.wait()
    store_middle.wait()
    store_coarse.wait()


def shards(counts, right_side, initial_guess, damping, group_map, block_inverse):
    bx, by, bz = right_side.shape
    f32 = jnp.float32
    vm = pltpu.VMEM

    def level_scratch(nx, ny, lanes, rounds):
        return [
            [vm((nx + 2, ny, lanes), f32)] * rounds,
            vm((rounds, 2, nx, lanes), f32), vm((rounds, 2, nx, lanes), f32),
            vm((rounds, ny, LANES), f32), vm((rounds, ny, LANES), f32),
        ]

    cx, cy, cz = counts
    mid = (bx // 2, by // 2, bz // 2)
    low = (bx // 4, by // 4, bz // 4)
    low_pad = (low[0], low[1], LANES)
    rows = low[0] * low[1]
    out_rows = block_inverse.shape[0]
    dma = pltpu.SemaphoreType.DMA
    any_space = pl.BlockSpec(memory_space=pl.ANY)
    in_hbm = pl.BlockSpec(memory_space=pltpu.HBM)
    outs = pl.pallas_call(
        functools.partial(kernel, counts),
        out_shape=(
            jax.ShapeDtypeStruct((bx, by, bz), f32),
            jax.ShapeDtypeStruct(mid, f32),
            jax.ShapeDtypeStruct(low, f32),
            jax.ShapeDtypeStruct((1, out_rows), f32),
        ),
        in_specs=[in_hbm] * 5,
        out_specs=(any_space, any_space, any_space, pl.BlockSpec(memory_space=pltpu.VMEM)),
        scratch_shapes=[
            *level_scratch(bx, by, bz, SWEEPS + 1),
            *level_scratch(*mid, SWEEPS),
            *level_scratch(*low_pad, SWEEPS),
            vm((bx, by, bz), f32), vm((bx, by, bz), f32), vm(low, jnp.int32), vm(block_inverse.shape, f32),
            vm((bx, by, bz), f32), vm((bx, by, bz), f32),
            vm(mid, f32), vm(mid, f32), vm(mid, f32), vm(mid, f32),
            vm(low_pad, f32), vm(low_pad, f32), vm(low_pad, f32), vm(low_pad, f32),
            vm((mid[0] * by, LANES), f32), vm((low[0] * mid[1], LANES), f32),
            vm((rows, LANES), f32), vm(low, f32), vm((rows, LANES), jnp.int32),
            vm((rows // 4, LANES, 2 * LANES), jnp.bfloat16),
            vm((cx * cz, NAGG // LANES, LANES), f32), vm((cy, NAGG // LANES, LANES), f32),
            dma((SWEEPS + 1, 5)), dma((SWEEPS + 1, 5)),
            dma((SWEEPS, 5)), dma((SWEEPS, 5)), dma((SWEEPS, 5)), dma((SWEEPS, 5)),
            dma((cx * cz,)), dma((cx * cz,)), dma((cy,)), dma((cy,)), dma((8,)),
        ],
        compiler_params=pltpu.CompilerParams(
            collective_id=0, has_side_effects=True, vmem_limit_bytes=48 * 1024 * 1024),
        cost_estimate=pl.CostEstimate(flops=40_000_000, bytes_accessed=6_000_000, transcendentals=0),
    )(right_side, initial_guess, damping, group_map, block_inverse)
    fine, middle, coarse, solved = outs
    return fine, middle, coarse, solved.reshape(out_rows)


def solution(mesh):
    counts = tuple(mesh.shape[axis] for axis in ("gx", "gy", "gz"))
    cells = P("gx", "gy", "gz")
    return jax.shard_map(
        functools.partial(shards, counts),
        mesh=mesh,
        in_specs=(cells, cells, cells, cells, P("gy", None)),
        out_specs=(cells, cells, cells, P("gy")),
        check_vma=False,
    )
```

```python
import functools
import math

import jax
import jax.numpy as jnp
from jax import lax
from jax.experimental import pallas as pl
from jax.experimental.pallas import tpu as pltpu
from jax.sharding import PartitionSpec as P

SWEEPS = 4
NAGG = 1024
OMEGA = 0.8
LANES = 128
MESH = pl.DeviceIdType.MESH


def split_dot(left, right_bf16, dims):
    high = left.astype(jnp.bfloat16)
    low = (left - high.astype(jnp.float32)).astype(jnp.bfloat16)
    out = lax.dot_general(high, right_bf16, dims, preferred_element_type=jnp.float32)
    return out + lax.dot_general(low, right_bf16, dims, preferred_element_type=jnp.float32)


def pair_matrix(rows, columns):
    row = lax.broadcasted_iota(jnp.int32, (rows, columns), 0)
    column = lax.broadcasted_iota(jnp.int32, (rows, columns), 1)
    first = jnp.where(row == 2 * column, 1.0, 0.0)
    return (first + jnp.where(row == 2 * column + 1, 1.0, 0.0)).astype(jnp.bfloat16)


class Level:
    def __init__(self, dims, lanes, fields, y_send, y_recv, z_send, z_recv, sems, place, counts):
        self.nx, self.ny, self.nz = dims
        self.lanes = lanes
        self.fields, self.y_send, self.y_recv = fields, y_send, y_recv
        self.z_send, self.z_recv = z_send, z_recv
        self.send_sem, self.recv_sem = sems
        self.gx, self.gy, self.gz = place
        self.counts = counts
        self.edge = jnp.where(self.gz == 0, self.nz - 1, 0)

    def clear(self):
        nx, ny, lanes = self.nx, self.ny, self.lanes
        rounds = len(self.fields)

        @pl.when(self.gx == 0)
        def _():
            for step in range(rounds):
                self.fields[step][0] = jnp.zeros((ny, lanes), jnp.float32)

        @pl.when(self.gx == self.counts[0] - 1)
        def _():
            for step in range(rounds):
                self.fields[step][nx + 1] = jnp.zeros((ny, lanes), jnp.float32)

        @pl.when(self.gy == 0)
        def _():
            for step in range(rounds):
                self.y_recv[step, 0] = jnp.zeros((nx, lanes), jnp.float32)

        @pl.when(self.gy == self.counts[1] - 1)
        def _():
            for step in range(rounds):
                self.y_recv[step, 1] = jnp.zeros((nx, lanes), jnp.float32)

        for step in range(rounds):
            self.z_send[step] = jnp.zeros((ny, LANES), jnp.float32)

    def x_copies(self, step, low=None, high=None):
        gx, gy, gz = self.gx, self.gy, self.gz
        field = self.fields[step]
        low = field.at[1] if low is None else low
        high = field.at[self.nx] if high is None else high
        up = pltpu.make_async_remote_copy(
            src_ref=high, dst_ref=field.at[0],
            send_sem=self.send_sem.at[step, 0], recv_sem=self.recv_sem.at[step, 0],
            device_id=(gx + 1, gy, gz), device_id_type=MESH)
        down = pltpu.make_async_remote_copy(
            src_ref=low, dst_ref=field.at[self.nx + 1],
            send_sem=self.send_sem.at[step, 1], recv_sem=self.recv_sem.at[step, 1],
            device_id=(gx - 1, gy, gz), device_id_type=MESH)
        return (gx, self.counts[0], up, down)

    def y_copies(self, step):
        gx, gy, gz = self.gx, self.gy, self.gz
        up = pltpu.make_async_remote_copy(
            src_ref=self.y_send.at[step, 1], dst_ref=self.y_recv.at[step, 0],
            send_sem=self.send_sem.at[step, 2], recv_sem=self.recv_sem.at[step, 2],
            device_id=(gx, gy + 1, gz), device_id_type=MESH)
        down = pltpu.make_async_remote_copy(
            src_ref=self.y_send.at[step, 0], dst_ref=self.y_recv.at[step, 1],
            send_sem=self.send_sem.at[step, 3], recv_sem=self.recv_sem.at[step, 3],
            device_id=(gx, gy - 1, gz), device_id_type=MESH)
        return (gy, self.counts[1], up, down)

    def z_copy(self, step):
        return pltpu.make_async_remote_copy(
            src_ref=self.z_send.at[step], dst_ref=self.z_recv.at[step],
            send_sem=self.send_sem.at[step, 4], recv_sem=self.recv_sem.at[step, 4],
            device_id=(self.gx, self.gy, 1 - self.gz), device_id_type=MESH)

    @staticmethod
    def start(copies):
        at, count, up, down = copies
        pl.when(at < count - 1)(up.start)
        pl.when(at > 0)(down.start)

    @staticmethod
    def wait_recv(copies):
        at, count, up, down = copies
        pl.when(at > 0)(up.wait_recv)
        pl.when(at < count - 1)(down.wait_recv)

    @staticmethod
    def wait_send(copies):
        at, count, up, down = copies
        pl.when(at < count - 1)(up.wait_send)
        pl.when(at > 0)(down.wait_send)

    def start_yz(self, step):
        self.z_copy(step).start()
        self.start(self.y_copies(step))

    def start_all(self, step):
        self.start(self.x_copies(step))
        self.start_yz(step)

    def wait_yz(self, step):
        self.wait_recv(self.y_copies(step))
        self.z_copy(step).wait_recv()

    def wait_x(self, step):
        self.wait_recv(self.x_copies(step))

    def wait_sends(self, step):
        self.wait_send(self.x_copies(step))
        self.wait_send(self.y_copies(step))
        self.z_copy(step).wait_send()

    def pack(self, step, x, value, face):
        ny, lanes = self.ny, self.lanes
        self.y_send[step, 0, pl.ds(x, 1), :] = value[0:1]
        self.y_send[step, 1, pl.ds(x, 1), :] = value[ny - 1:ny]
        if lanes > LANES:
            tile = jnp.where(self.gz == 0, value[:, lanes - LANES:], value[:, :LANES])
        else:
            tile = value
        edge = lax.rem(self.edge, LANES)
        turned = pltpu.roll(tile, lax.rem(x - edge + LANES, LANES), 1)
        lane = lax.broadcasted_iota(jnp.int32, (ny, LANES), 1)
        return jnp.where(lane == x, turned, face)

    def around(self, step, x):
        ny, lanes = self.ny, self.lanes
        field = self.fields[step]
        value = field[x + 1]
        below = self.y_recv[step, 0, pl.ds(x, 1), :]
        above = self.y_recv[step, 1, pl.ds(x, 1), :]
        total = field[x] + field[x + 2]
        total = total + jnp.concatenate([below, value[:ny - 1]], axis=0)
        total = total + jnp.concatenate([value[1:], above], axis=0)
        lane = lax.broadcasted_iota(jnp.int32, (ny, LANES), 1)
        face = pltpu.roll(self.z_recv[step], lax.rem(lax.rem(self.edge, LANES) - x + LANES, LANES), 1)
        left_face = jnp.where(self.gz == 0, 0.0, face)
        right_face = jnp.where(self.gz == 0, face, 0.0)
        tiles = [value[:, at:at + LANES] for at in range(0, lanes, LANES)]
        lefts = [left_face] + [pltpu.roll(tile, 1, 1) for tile in tiles]
        rights = [pltpu.roll(tile, LANES - 1, 1) for tile in tiles] + [right_face]
        sides = []
        for at in range(len(tiles)):
            right = rights[at]
            if at + 1 < len(tiles) or self.nz == lanes:
                right = jnp.where(lane == LANES - 1, rights[at + 1], right)
            else:
                right = jnp.where(lane == self.nz - 1, right_face, right)
            sides.append(jnp.where(lane == 0, lefts[at], lefts[at + 1]) + right)
        around = sides[0] if len(sides) == 1 else jnp.concatenate(sides, axis=1)
        return value, total + around


def kernel(counts, rhs_hbm, guess_hbm, damp_hbm, group_hbm, inverse_hbm,
           fine_hbm, middle_hbm, coarse_hbm, solved_ref,
           f_fields, f_ys, f_yr, f_zs, f_zr,
           m_fields, m_ys, m_yr, m_zs, m_zr,
           c_fields, c_ys, c_yr, c_zs, c_zr,
           rhs, damp, group, inverse, weight, scaled,
           m_damp, m_src, m_weight, m_scaled, c_damp, c_src, c_weight, c_scaled,
           halves, quarters, c_defect, c_out, group_rows, onehot, reduced, gathered,
           f_send, f_recv, m_send, m_recv, c_send, c_recv,
           r_send, r_recv, g_send, g_recv, local_sem):
    place = gx, gy, gz = lax.axis_index("gx"), lax.axis_index("gy"), lax.axis_index("gz")
    cx, cy, cz = counts
    bx, by, bz = rhs.shape
    fine = Level((bx, by, bz), bz, f_fields, f_ys, f_yr, f_zs, f_zr, (f_send, f_recv), place, counts)
    middle = Level((bx // 2, by // 2, bz // 2), bz // 2, m_fields, m_ys, m_yr, m_zs, m_zr,
                   (m_send, m_recv), place, counts)
    coarse = Level((bx // 4, by // 4, bz // 4), LANES, c_fields, c_ys, c_yr, c_zs, c_zr,
                   (c_send, c_recv), place, counts)

    loads = [
        pltpu.make_async_copy(guess_hbm, f_fields[0].at[pl.ds(1, bx)], local_sem.at[0]),
        pltpu.make_async_copy(damp_hbm, damp, local_sem.at[1]),
        pltpu.make_async_copy(rhs_hbm, rhs, local_sem.at[2]),
        pltpu.make_async_copy(group_hbm, group, local_sem.at[3]),
        pltpu.make_async_copy(inverse_hbm, inverse, local_sem.at[4]),
    ]
    for load in loads:
        load.start()

    mates = [(i, k) for i in range(cx) for k in range(cz)]
    barrier = pltpu.get_barrier_semaphore()
    for i, k in mates:
        @pl.when(jnp.logical_or(gx != i, gz != k))
        def _():
            pl.semaphore_signal(barrier, inc=1, device_id=(i, gy, k), device_id_type=MESH)
    for j in range(cy):
        @pl.when(gy != j)
        def _():
            pl.semaphore_signal(barrier, inc=1, device_id=(gx, j, gz), device_id_type=MESH)

    for level in (fine, middle, coarse):
        level.clear()
    pl.semaphore_wait(barrier, len(mates) - 1 + cy - 1)

    first_x = fine.x_copies(0, guess_hbm.at[0], guess_hbm.at[bx - 1])
    fine.start(first_x)
    loads[0].wait()

    @pl.loop(0, bx // 4)
    def _(group):
        face = f_zs[0]
        for part in range(4):
            x = group * 4 + part
            face = fine.pack(0, x, f_fields[0][x + 1], face)
        f_zs[0] = face

    fine.start_yz(0)

    loads[1].wait()
    loads[2].wait()
    pair_fine = pair_matrix(bz, bz // 2)
    pair_middle = pair_matrix(bz // 2, LANES)

    @pl.loop(0, bx, unroll=4)
    def _(x):
        factor = OMEGA / (6.0 + damp[x])
        weight[x] = factor
        scaled[x] = factor * rhs[x]

    def shrink_to(source, target, scratch, pairs, nx, ny):
        for x in range(nx):
            both = source(2 * x) + source(2 * x + 1)
            scratch[pl.ds(x * 2 * ny, 2 * ny), :] = split_dot(both, pairs, (((1,), (0,)), ((), ())))
        for x in range(nx):
            even = scratch[pl.ds(x * 2 * ny, ny, stride=2), :]
            odd = scratch[pl.ds(x * 2 * ny + 1, ny, stride=2), :]
            target[x] = 0.5 * (even + odd)

    shrink_to(lambda x: damp[x], m_damp, halves, pair_fine, middle.nx, middle.ny)
    shrink_to(lambda x: m_damp[x], c_damp, quarters, pair_middle, coarse.nx, coarse.ny)
    c_lane = lax.broadcasted_iota(jnp.int32, (coarse.nx, coarse.ny, LANES), 2)
    m_weight[...] = OMEGA / (6.0 + m_damp[...])
    c_weight[...] = jnp.where(c_lane < coarse.nz, OMEGA / (6.0 + c_damp[...]), 0.0)

    loads[3].wait()
    rows = coarse.nx * coarse.ny
    cells = coarse.nz
    group_rows[...] = jnp.zeros((rows, LANES), jnp.int32)
    for x in range(coarse.nx):
        group_rows[pl.ds(x * coarse.ny, coarse.ny), pl.ds(0, cells)] = group[x]
    packed = group_rows[pl.ds(0, rows // 2), :]
    packed = packed + pltpu.roll(group_rows[pl.ds(rows // 2, rows // 2), :], cells, 1)
    group_rows[pl.ds(0, rows // 2), :] = packed
    half = rows // 4

    @pl.loop(0, half, unroll=4)
    def _(row):
        number = lax.broadcasted_iota(jnp.int32, (LANES, LANES), 0)
        for part in range(2):
            low = group_rows[pl.ds(row + part * half, 1), :] & (LANES - 1)
            onehot[row, :, part * LANES:(part + 1) * LANES] = jnp.where(
                number == low, 1.0, 0.0).astype(jnp.bfloat16)

    def sweep(level, step, weights, scaleds, planes):
        def one(x, face):
            value, total = level.around(step, x)
            new = (1.0 - OMEGA) * value + (scaleds[x] + weights[x] * total)
            level.fields[step + 1][x + 1] = new
            return level.pack(step + 1, x, new, face)

        level.wait_yz(step)
        size = 2 if planes > 8 else planes - 2

        def some(first):
            face = level.z_send[step + 1]
            for part in range(size):
                face = one(first + part, face)
            level.z_send[step + 1] = face

        if size == planes - 2:
            some(1)
        else:
            @pl.loop(0, (planes - 2) // size)
            def _(group):
                some(group * size + 1)

        level.wait_x(step)
        face = one(0, level.z_send[step + 1])
        face = one(planes - 1, face)
        level.start(level.x_copies(step + 1))
        level.z_send[step + 1] = face
        level.start_yz(step + 1)

    for step in range(SWEEPS):
        sweep(fine, step, weight, scaled, bx)
    store_fine = pltpu.make_async_copy(f_fields[SWEEPS].at[pl.ds(1, bx)], fine_hbm, local_sem.at[5])
    store_fine.start()

    fine.wait_yz(SWEEPS)

    def defect_pair(x):
        total = None
        for plane in (2 * x, 2 * x + 1):
            value, around = fine.around(SWEEPS, plane)
            part = rhs[plane] - ((6.0 + damp[plane]) * value - around)
            total = part if total is None else total + part
        halves[pl.ds(pl.multiple_of(x * by, by), by), :] = split_dot(total, pair_fine, (((1,), (0,)), ((), ())))

    @pl.loop(1, middle.nx - 1, unroll=2)
    def _(x):
        defect_pair(x)

    fine.wait_x(SWEEPS)
    defect_pair(0)
    defect_pair(middle.nx - 1)

    def enter(level, scratch, source, weights, scaleds):
        ny = level.ny
        face = jnp.zeros((ny, LANES), jnp.float32)
        for x in range(level.nx):
            even = scratch[pl.ds(x * 2 * ny, ny, stride=2), :]
            odd = scratch[pl.ds(x * 2 * ny + 1, ny, stride=2), :]
            source[x] = 0.5 * (even + odd)
            new = weights[x] * source[x]
            scaleds[x] = new
            level.fields[0][x + 1] = new
            face = level.pack(0, x, new, face)
        level.z_send[0] = face
        level.start_all(0)

    enter(middle, halves, m_src, m_weight, m_scaled)
    for step in range(SWEEPS - 1):
        sweep(middle, step, m_weight, m_scaled, middle.nx)
    last = SWEEPS - 1
    store_middle = pltpu.make_async_copy(m_fields[last].at[pl.ds(1, middle.nx)], middle_hbm, local_sem.at[6])
    store_middle.start()
    middle.wait_yz(last)
    middle.wait_x(last)

    my = middle.ny
    for x in range(coarse.nx):
        total = None
        for plane in (2 * x, 2 * x + 1):
            value, around = middle.around(last, plane)
            part = m_src[plane] - ((6.0 + m_damp[plane]) * value - around)
            total = part if total is None else total + part
        quarters[pl.ds(x * my, my), :] = split_dot(total, pair_middle, (((1,), (0,)), ((), ())))

    enter(coarse, quarters, c_src, c_weight, c_scaled)
    for step in range(SWEEPS - 1):
        sweep(coarse, step, c_weight, c_scaled, coarse.nx)
    for x in range(coarse.nx):
        c_out[x] = c_fields[last][x + 1][:, :cells]
    store_coarse = pltpu.make_async_copy(c_out, coarse_hbm, local_sem.at[7])
    store_coarse.start()
    coarse.wait_yz(last)
    coarse.wait_x(last)
    valid = lax.broadcasted_iota(jnp.int32, (coarse.ny, LANES), 1) < cells
    for x in range(coarse.nx):
        value, around = coarse.around(last, x)
        part = c_src[x] - ((6.0 + c_damp[x]) * value - around)
        c_defect[pl.ds(x * coarse.ny, coarse.ny), :] = jnp.where(valid, part, 0.0)

    packed = c_defect[pl.ds(0, rows // 2), :]
    packed = packed + pltpu.roll(c_defect[pl.ds(rows // 2, rows // 2), :], cells, 1)
    c_defect[pl.ds(0, rows // 2), :] = packed

    tall = NAGG // LANES

    def gather_row(row, total):
        number = lax.broadcasted_iota(jnp.int32, (tall, LANES), 0)
        parts = []
        for part in range(2):
            at = pl.ds(row + part * half, 1)
            high = group_rows[at, :] // LANES
            parts.append(jnp.where(number == high, c_defect[at, :], 0.0))
        values = jnp.concatenate(parts, axis=1)
        first = values.astype(jnp.bfloat16).astype(jnp.float32)
        both = jnp.concatenate([first, values - first], axis=0).astype(jnp.bfloat16)
        return total + lax.dot_general(both, onehot[row], (((1,), (1,)), ((), ())),
                                       preferred_element_type=jnp.float32)

    sums = lax.fori_loop(0, half, gather_row, jnp.zeros((2 * tall, LANES), jnp.float32),
                         unroll=4)
    mine = gx * cz + gz
    reduced[mine] = sums[:tall] + sums[tall:]

    def reduce_copy(i, k):
        return pltpu.make_async_remote_copy(
            src_ref=reduced.at[mine], dst_ref=reduced.at[mine],
            send_sem=r_send.at[i * cz + k], recv_sem=r_recv.at[mine],
            device_id=(i, gy, k), device_id_type=MESH)

    def reduce_wait(i, k):
        return pltpu.make_async_remote_copy(
            src_ref=reduced.at[i * cz + k], dst_ref=reduced.at[i * cz + k],
            send_sem=r_send.at[i * cz + k], recv_sem=r_recv.at[i * cz + k],
            device_id=(i, gy, k), device_id_type=MESH)

    def mates_do(act):
        for i, k in mates:
            pl.when(jnp.logical_or(gx != i, gz != k))(functools.partial(act, i, k))

    mates_do(lambda i, k: reduce_copy(i, k).start())
    mates_do(lambda i, k: reduce_wait(i, k).wait_recv())
    gathered[gy] = jnp.sum(reduced[...], axis=0)

    def gather_copy(j, slot, recv):
        return pltpu.make_async_remote_copy(
            src_ref=gathered.at[slot], dst_ref=gathered.at[slot],
            send_sem=g_send.at[j], recv_sem=g_recv.at[recv],
            device_id=(gx, j, gz), device_id_type=MESH)

    for j in range(cy):
        pl.when(gy != j)(lambda j=j: gather_copy(j, gy, gy).start())
    for j in range(cy):
        pl.when(gy != j)(lambda j=j: gather_copy(j, j, j).wait_recv())
    total_cells = rows * cells * cx * cy * cz
    source = jnp.sum(gathered[...], axis=0) * (1.0 / math.sqrt(total_cells // NAGG))

    loads[4].wait()
    out_rows = inverse.shape[0]
    product = None
    for part in range(tall):
        term = inverse[:, part * LANES:(part + 1) * LANES] * source[part:part + 1]
        product = term if product is None else product + term
    ones = jnp.ones((8, LANES), jnp.float32)
    solved = lax.dot_general(ones, product, (((1,), (1,)), ((), ())),
                             precision=lax.Precision.HIGHEST, preferred_element_type=jnp.float32)
    solved_ref[...] = solved[0:1]

    for step in range(SWEEPS + 1):
        if step == 0:
            fine.wait_send(first_x)
            fine.wait_send(fine.y_copies(0))
            fine.z_copy(0).wait_send()
        else:
            fine.wait_sends(step)
    for step in range(SWEEPS):
        middle.wait_sends(step)
        coarse.wait_sends(step)
    mates_do(lambda i, k: reduce_copy(i, k).wait_send())
    for j in range(cy):
        pl.when(gy != j)(lambda j=j: gather_copy(j, gy, gy).wait_send())
    store_fine.wait()
    store_middle.wait()
    store_coarse.wait()


def shards(counts, right_side, initial_guess, damping, group_map, block_inverse):
    bx, by, bz = right_side.shape
    f32 = jnp.float32
    vm = pltpu.VMEM

    def level_scratch(nx, ny, lanes, rounds):
        return [
            [vm((nx + 2, ny, lanes), f32)] * rounds,
            vm((rounds, 2, nx, lanes), f32), vm((rounds, 2, nx, lanes), f32),
            vm((rounds, ny, LANES), f32), vm((rounds, ny, LANES), f32),
        ]

    cx, cy, cz = counts
    mid = (bx // 2, by // 2, bz // 2)
    low = (bx // 4, by // 4, bz // 4)
    low_pad = (low[0], low[1], LANES)
    rows = low[0] * low[1]
    out_rows = block_inverse.shape[0]
    dma = pltpu.SemaphoreType.DMA
    any_space = pl.BlockSpec(memory_space=pl.ANY)
    in_hbm = pl.BlockSpec(memory_space=pltpu.HBM)
    outs = pl.pallas_call(
        functools.partial(kernel, counts),
        out_shape=(
            jax.ShapeDtypeStruct((bx, by, bz), f32),
            jax.ShapeDtypeStruct(mid, f32),
            jax.ShapeDtypeStruct(low, f32),
            jax.ShapeDtypeStruct((1, out_rows), f32),
        ),
        in_specs=[in_hbm] * 5,
        out_specs=(any_space, any_space, any_space, pl.BlockSpec(memory_space=pltpu.VMEM)),
        scratch_shapes=[
            *level_scratch(bx, by, bz, SWEEPS + 1),
            *level_scratch(*mid, SWEEPS),
            *level_scratch(*low_pad, SWEEPS),
            vm((bx, by, bz), f32), vm((bx, by, bz), f32), vm(low, jnp.int32), vm(block_inverse.shape, f32),
            vm((bx, by, bz), f32), vm((bx, by, bz), f32),
            vm(mid, f32), vm(mid, f32), vm(mid, f32), vm(mid, f32),
            vm(low_pad, f32), vm(low_pad, f32), vm(low_pad, f32), vm(low_pad, f32),
            vm((mid[0] * by, LANES), f32), vm((low[0] * mid[1], LANES), f32),
            vm((rows, LANES), f32), vm(low, f32), vm((rows, LANES), jnp.int32),
            vm((rows // 4, LANES, 2 * LANES), jnp.bfloat16),
            vm((cx * cz, NAGG // LANES, LANES), f32), vm((cy, NAGG // LANES, LANES), f32),
            dma((SWEEPS + 1, 5)), dma((SWEEPS + 1, 5)),
            dma((SWEEPS, 5)), dma((SWEEPS, 5)), dma((SWEEPS, 5)), dma((SWEEPS, 5)),
            dma((cx * cz,)), dma((cx * cz,)), dma((cy,)), dma((cy,)), dma((8,)),
        ],
        compiler_params=pltpu.CompilerParams(
            collective_id=0, has_side_effects=True, vmem_limit_bytes=63 * 1024 * 1024),
        cost_estimate=pl.CostEstimate(flops=40_000_000, bytes_accessed=6_000_000, transcendentals=0),
    )(right_side, initial_guess, damping, group_map, block_inverse)
    fine, middle, coarse, solved = outs
    return fine, middle, coarse, solved.reshape(out_rows)


def solution(mesh):
    counts = tuple(mesh.shape[axis] for axis in ("gx", "gy", "gz"))
    cells = P("gx", "gy", "gz")
    return jax.shard_map(
        functools.partial(shards, counts),
        mesh=mesh,
        in_specs=(cells, cells, cells, cells, P("gy", None)),
        out_specs=(cells, cells, cells, P("gy")),
        check_vma=False,
    )
```

```python
import functools
import math

import jax
import jax.numpy as jnp
from jax import lax
from jax.experimental import pallas as pl
from jax.experimental.pallas import tpu as pltpu
from jax.sharding import PartitionSpec as P

SWEEPS = 4
NAGG = 1024
OMEGA = 0.8
LANES = 128
MARGIN = 8
MESH = pl.DeviceIdType.MESH


def split_dot(left, right_bf16, dims):
    high = left.astype(jnp.bfloat16)
    low = (left - high.astype(jnp.float32)).astype(jnp.bfloat16)
    out = lax.dot_general(high, right_bf16, dims, preferred_element_type=jnp.float32)
    return out + lax.dot_general(low, right_bf16, dims, preferred_element_type=jnp.float32)


def pair_matrix(rows, columns):
    row = lax.broadcasted_iota(jnp.int32, (rows, columns), 0)
    column = lax.broadcasted_iota(jnp.int32, (rows, columns), 1)
    first = jnp.where(row == 2 * column, 1.0, 0.0)
    return (first + jnp.where(row == 2 * column + 1, 1.0, 0.0)).astype(jnp.bfloat16)


class Level:
    def __init__(self, dims, lanes, fields, y_send, y_recv, z_send, z_recv, sems, place, counts):
        self.nx, self.ny, self.nz = dims
        self.lanes = lanes
        self.fields, self.y_send, self.y_recv = fields, y_send, y_recv
        self.z_send, self.z_recv = z_send, z_recv
        self.send_sem, self.recv_sem = sems
        self.gx, self.gy, self.gz = place
        self.counts = counts
        self.edge = jnp.where(self.gz == 0, self.nz - 1, 0)

    def clear(self):
        nx, ny, lanes = self.nx, self.ny, self.lanes
        rounds = len(self.fields)

        @pl.when(self.gx == 0)
        def _():
            for step in range(rounds):
                self.fields[step][0] = jnp.zeros((ny, lanes), jnp.float32)

        @pl.when(self.gx == self.counts[0] - 1)
        def _():
            for step in range(rounds):
                self.fields[step][nx + 1] = jnp.zeros((ny, lanes), jnp.float32)

        @pl.when(self.gy == 0)
        def _():
            for step in range(rounds):
                self.y_recv[step, 0] = jnp.zeros((nx, lanes), jnp.float32)

        @pl.when(self.gy == self.counts[1] - 1)
        def _():
            for step in range(rounds):
                self.y_recv[step, 1] = jnp.zeros((nx, lanes), jnp.float32)

        for step in range(rounds):
            self.z_send[step] = jnp.zeros((ny, LANES), jnp.float32)

    def x_copies(self, step, low=None, high=None):
        gx, gy, gz = self.gx, self.gy, self.gz
        field = self.fields[step]
        low = field.at[1] if low is None else low
        high = field.at[self.nx] if high is None else high
        up = pltpu.make_async_remote_copy(
            src_ref=high, dst_ref=field.at[0],
            send_sem=self.send_sem.at[step, 0], recv_sem=self.recv_sem.at[step, 0],
            device_id=(gx + 1, gy, gz), device_id_type=MESH)
        down = pltpu.make_async_remote_copy(
            src_ref=low, dst_ref=field.at[self.nx + 1],
            send_sem=self.send_sem.at[step, 1], recv_sem=self.recv_sem.at[step, 1],
            device_id=(gx - 1, gy, gz), device_id_type=MESH)
        return (gx, self.counts[0], up, down)

    def y_copies(self, step):
        gx, gy, gz = self.gx, self.gy, self.gz
        up = pltpu.make_async_remote_copy(
            src_ref=self.y_send.at[step, 1], dst_ref=self.y_recv.at[step, 0],
            send_sem=self.send_sem.at[step, 2], recv_sem=self.recv_sem.at[step, 2],
            device_id=(gx, gy + 1, gz), device_id_type=MESH)
        down = pltpu.make_async_remote_copy(
            src_ref=self.y_send.at[step, 0], dst_ref=self.y_recv.at[step, 1],
            send_sem=self.send_sem.at[step, 3], recv_sem=self.recv_sem.at[step, 3],
            device_id=(gx, gy - 1, gz), device_id_type=MESH)
        return (gy, self.counts[1], up, down)

    def z_copy(self, step):
        return pltpu.make_async_remote_copy(
            src_ref=self.z_send.at[step], dst_ref=self.z_recv.at[step],
            send_sem=self.send_sem.at[step, 4], recv_sem=self.recv_sem.at[step, 4],
            device_id=(self.gx, self.gy, 1 - self.gz), device_id_type=MESH)

    @staticmethod
    def start(copies):
        at, count, up, down = copies
        pl.when(at < count - 1)(up.start)
        pl.when(at > 0)(down.start)

    @staticmethod
    def wait_recv(copies):
        at, count, up, down = copies
        pl.when(at > 0)(up.wait_recv)
        pl.when(at < count - 1)(down.wait_recv)

    @staticmethod
    def wait_send(copies):
        at, count, up, down = copies
        pl.when(at < count - 1)(up.wait_send)
        pl.when(at > 0)(down.wait_send)

    def start_yz(self, step):
        self.z_copy(step).start()
        self.start(self.y_copies(step))

    def start_all(self, step):
        self.start(self.x_copies(step))
        self.start_yz(step)

    def wait_yz(self, step):
        self.wait_recv(self.y_copies(step))
        self.z_copy(step).wait_recv()

    def wait_x(self, step):
        self.wait_recv(self.x_copies(step))

    def wait_sends(self, step):
        self.wait_send(self.x_copies(step))
        self.wait_send(self.y_copies(step))
        self.z_copy(step).wait_send()

    def pack(self, step, x, value, face):
        ny, lanes = self.ny, self.lanes
        self.y_send[step, 0, pl.ds(x, 1), :] = value[0:1]
        self.y_send[step, 1, pl.ds(x, 1), :] = value[ny - 1:ny]
        if lanes > LANES:
            tile = jnp.where(self.gz == 0, value[:, lanes - LANES:], value[:, :LANES])
        else:
            tile = value
        edge = lax.rem(self.edge, LANES)
        turned = pltpu.roll(tile, lax.rem(x - edge + LANES, LANES), 1)
        lane = lax.broadcasted_iota(jnp.int32, (ny, LANES), 1)
        return jnp.where(lane == x, turned, face)

    def around(self, step, x):
        ny, lanes = self.ny, self.lanes
        field = self.fields[step]
        value = field[x + 1]
        below = self.y_recv[step, 0, pl.ds(x, 1), :]
        above = self.y_recv[step, 1, pl.ds(x, 1), :]
        total = field[x] + field[x + 2]
        total = total + jnp.concatenate([below, value[:ny - 1]], axis=0)
        total = total + jnp.concatenate([value[1:], above], axis=0)
        lane = lax.broadcasted_iota(jnp.int32, (ny, LANES), 1)
        face = pltpu.roll(self.z_recv[step], lax.rem(lax.rem(self.edge, LANES) - x + LANES, LANES), 1)
        left_face = jnp.where(self.gz == 0, 0.0, face)
        right_face = jnp.where(self.gz == 0, face, 0.0)
        tiles = [value[:, at:at + LANES] for at in range(0, lanes, LANES)]
        lefts = [left_face] + [pltpu.roll(tile, 1, 1) for tile in tiles]
        rights = [pltpu.roll(tile, LANES - 1, 1) for tile in tiles] + [right_face]
        sides = []
        for at in range(len(tiles)):
            right = rights[at]
            if at + 1 < len(tiles) or self.nz == lanes:
                right = jnp.where(lane == LANES - 1, rights[at + 1], right)
            else:
                right = jnp.where(lane == self.nz - 1, right_face, right)
            sides.append(jnp.where(lane == 0, lefts[at], lefts[at + 1]) + right)
        around = sides[0] if len(sides) == 1 else jnp.concatenate(sides, axis=1)
        return value, total + around


class Deep:
    def __init__(self, dims, fields, wide, half, half_in, full, z_sems, d_sems, place, counts):
        self.nx, self.ny, self.nz = dims
        self.fields, self.wide = fields, wide
        self.half, self.half_in, self.full = half, half_in, full
        self.z_sems, self.d_sems = z_sems, d_sems
        self.gx, self.gy, self.gz = place
        self.counts = counts
        self.ways = [(i, j) for i in (-1, 0, 1) for j in (-1, 0, 1) if (i, j) != (0, 0)]

    def there(self, i, j):
        here = jnp.bool_(True)
        for at, count, step in ((self.gx, self.counts[0], i), (self.gy, self.counts[1], j)):
            if step == 1:
                here = jnp.logical_and(here, at < count - 1)
            if step == -1:
                here = jnp.logical_and(here, at > 0)
        return here

    def place_of(self, i, j):
        low = {-1: 0, 0: MARGIN, 1: MARGIN + self.ny}[j]
        return pl.ds((1 + i) * self.nx, self.nx), pl.ds(low, self.ny if j == 0 else MARGIN)

    def corners(self):
        beside = [jnp.where(self.there(i, j), 1, 0) for i, j in self.ways if i and j]
        return sum(beside)

    def greet(self, barrier):
        for i, j in self.ways:
            if i and j:
                @pl.when(self.there(i, j))
                def _():
                    pl.semaphore_signal(barrier, inc=1, device_id=(self.gx + i, self.gy + j, self.gz),
                                        device_id_type=MESH)

    def clear(self):
        for i, j in self.ways:
            planes, rows = self.place_of(i, j)

            @pl.when(jnp.logical_not(self.there(i, j)))
            def _():
                for kind in range(2):
                    self.wide[kind, planes, rows, :] = jnp.zeros((planes.size, rows.size, LANES), jnp.float32)

    def z_copy(self, kind):
        return pltpu.make_async_remote_copy(
            src_ref=self.half.at[kind], dst_ref=self.half_in.at[kind],
            send_sem=self.z_sems[0].at[kind], recv_sem=self.z_sems[1].at[kind],
            device_id=(self.gx, self.gy, 1 - self.gz), device_id_type=MESH)

    def merge(self, kind, block):
        for x in range(self.nx):
            self.half[kind, x] = pltpu.roll(block[x], self.gz * self.nz, 1)
        self.z_copy(kind).start()

    def d_copy(self, kind, i, j):
        planes, rows = self.place_of(-i, -j)
        first = self.ny - MARGIN if j == 1 else 0
        way = (i + 1) * 3 + j + 1
        return pltpu.make_async_remote_copy(
            src_ref=self.full.at[kind, :, pl.ds(first, rows.size)],
            dst_ref=self.wide.at[kind, planes, rows],
            send_sem=self.d_sems[0].at[kind, way], recv_sem=self.d_sems[1].at[kind, way],
            device_id=(self.gx + i, self.gy + j, self.gz), device_id_type=MESH)

    def spread(self, kind):
        self.z_copy(kind).wait_recv()
        self.full[kind] = self.half[kind] + self.half_in[kind]
        for i, j in self.ways:
            pl.when(self.there(i, j))(self.d_copy(kind, i, j).start)
        planes, rows = self.place_of(0, 0)
        self.wide[kind, planes, rows, :] = self.full[kind]

    def collect(self, kind):
        for i, j in self.ways:
            pl.when(self.there(-i, -j))(self.d_copy(kind, i, j).wait_recv)

    def wait_sends(self):
        for kind in range(2):
            self.z_copy(kind).wait_send()
            for i, j in self.ways:
                pl.when(self.there(i, j))(self.d_copy(kind, i, j).wait_send)

    def own(self, plane):
        return pltpu.roll(plane[MARGIN:MARGIN + self.ny], self.gz * self.nz, 1)

    def around(self, step, x):
        field = self.fields[step]
        value = field[x]
        rows = value.shape[0]
        lane = lax.broadcasted_iota(jnp.int32, value.shape, 1)
        total = field[x - 1] + field[x + 1]
        total = total + pltpu.roll(value, 1, 0) + pltpu.roll(value, rows - 1, 0)
        total = total + jnp.where(lane == 0, 0.0, pltpu.roll(value, 1, 1))
        return value, total + jnp.where(lane == LANES - 1, 0.0, pltpu.roll(value, LANES - 1, 1))

    def smooth(self):
        planes = 3 * self.nx
        for x in range(planes):
            self.fields[0][x] = self.wide[0, x] * self.wide[1, x]
        for step in range(1, SWEEPS):
            for x in range(step, planes - step):
                value, total = self.around(step - 1, x)
                self.fields[step][x] = (1.0 - OMEGA) * value + self.wide[0, x] * (self.wide[1, x] + total)


def kernel(counts, rhs_hbm, guess_hbm, damp_hbm, group_hbm, inverse_hbm,
           fine_hbm, middle_hbm, coarse_hbm, solved_ref,
           f_fields, f_ys, f_yr, f_zs, f_zr,
           m_fields, m_ys, m_yr, m_zs, m_zr,
           c_fields, deep, half, half_in, full,
           rhs, damp, group, inverse, weight, scaled,
           m_damp, m_src, m_weight, m_scaled, c_damp, c_src,
           halves, quarters, c_defect, c_out, group_rows, onehot, reduced, gathered,
           f_send, f_recv, m_send, m_recv, hz_send, hz_recv, d_send, d_recv,
           r_send, r_recv, g_send, g_recv, local_sem):
    place = gx, gy, gz = lax.axis_index("gx"), lax.axis_index("gy"), lax.axis_index("gz")
    cx, cy, cz = counts
    bx, by, bz = rhs.shape
    fine = Level((bx, by, bz), bz, f_fields, f_ys, f_yr, f_zs, f_zr, (f_send, f_recv), place, counts)
    middle = Level((bx // 2, by // 2, bz // 2), bz // 2, m_fields, m_ys, m_yr, m_zs, m_zr,
                   (m_send, m_recv), place, counts)
    coarse = Deep((bx // 4, by // 4, bz // 4), c_fields, deep, half, half_in, full,
                  (hz_send, hz_recv), (d_send, d_recv), place, counts)

    loads = [
        pltpu.make_async_copy(guess_hbm, f_fields[0].at[pl.ds(1, bx)], local_sem.at[0]),
        pltpu.make_async_copy(damp_hbm, damp, local_sem.at[1]),
        pltpu.make_async_copy(rhs_hbm, rhs, local_sem.at[2]),
        pltpu.make_async_copy(group_hbm, group, local_sem.at[3]),
        pltpu.make_async_copy(inverse_hbm, inverse, local_sem.at[4]),
    ]
    for load in loads:
        load.start()

    mates = [(i, k) for i in range(cx) for k in range(cz)]
    barrier = pltpu.get_barrier_semaphore()
    for i, k in mates:
        @pl.when(jnp.logical_or(gx != i, gz != k))
        def _():
            pl.semaphore_signal(barrier, inc=1, device_id=(i, gy, k), device_id_type=MESH)
    for j in range(cy):
        @pl.when(gy != j)
        def _():
            pl.semaphore_signal(barrier, inc=1, device_id=(gx, j, gz), device_id_type=MESH)

    coarse.greet(barrier)
    for level in (fine, middle, coarse):
        level.clear()
    pl.semaphore_wait(barrier, len(mates) - 1 + cy - 1 + coarse.corners())

    first_x = fine.x_copies(0, guess_hbm.at[0], guess_hbm.at[bx - 1])
    fine.start(first_x)
    loads[0].wait()

    @pl.loop(0, bx // 4)
    def _(group):
        face = f_zs[0]
        for part in range(4):
            x = group * 4 + part
            face = fine.pack(0, x, f_fields[0][x + 1], face)
        f_zs[0] = face

    fine.start_yz(0)

    loads[1].wait()
    loads[2].wait()
    pair_fine = pair_matrix(bz, bz // 2)
    pair_middle = pair_matrix(bz // 2, LANES)

    @pl.loop(0, bx, unroll=4)
    def _(x):
        factor = OMEGA / (6.0 + damp[x])
        weight[x] = factor
        scaled[x] = factor * rhs[x]

    def shrink_to(source, target, scratch, pairs, nx, ny):
        for x in range(nx):
            both = source(2 * x) + source(2 * x + 1)
            scratch[pl.ds(x * 2 * ny, 2 * ny), :] = split_dot(both, pairs, (((1,), (0,)), ((), ())))
        for x in range(nx):
            even = scratch[pl.ds(x * 2 * ny, ny, stride=2), :]
            odd = scratch[pl.ds(x * 2 * ny + 1, ny, stride=2), :]
            target[x] = 0.5 * (even + odd)

    shrink_to(lambda x: damp[x], m_damp, halves, pair_fine, middle.nx, middle.ny)
    shrink_to(lambda x: m_damp[x], c_damp, quarters, pair_middle, coarse.nx, coarse.ny)
    c_lane = lax.broadcasted_iota(jnp.int32, (coarse.nx, coarse.ny, LANES), 2)
    m_weight[...] = OMEGA / (6.0 + m_damp[...])
    coarse.merge(0, jnp.where(c_lane < coarse.nz, OMEGA / (6.0 + c_damp[...]), 0.0))

    loads[3].wait()
    rows = coarse.nx * coarse.ny
    cells = coarse.nz
    group_rows[...] = jnp.zeros((rows, LANES), jnp.int32)
    for x in range(coarse.nx):
        group_rows[pl.ds(x * coarse.ny, coarse.ny), pl.ds(0, cells)] = group[x]
    packed = group_rows[pl.ds(0, rows // 2), :]
    packed = packed + pltpu.roll(group_rows[pl.ds(rows // 2, rows // 2), :], cells, 1)
    group_rows[pl.ds(0, rows // 2), :] = packed
    half = rows // 4

    @pl.loop(0, half, unroll=4)
    def _(row):
        number = lax.broadcasted_iota(jnp.int32, (LANES, LANES), 0)
        for part in range(2):
            low = group_rows[pl.ds(row + part * half, 1), :] & (LANES - 1)
            onehot[row, :, part * LANES:(part + 1) * LANES] = jnp.where(
                number == low, 1.0, 0.0).astype(jnp.bfloat16)

    def sweep(level, step, weights, scaleds, planes):
        def one(x, face):
            value, total = level.around(step, x)
            new = (1.0 - OMEGA) * value + (scaleds[x] + weights[x] * total)
            level.fields[step + 1][x + 1] = new
            return level.pack(step + 1, x, new, face)

        level.wait_yz(step)
        size = 2 if planes > 8 else planes - 2

        def some(first):
            face = level.z_send[step + 1]
            for part in range(size):
                face = one(first + part, face)
            level.z_send[step + 1] = face

        if size == planes - 2:
            some(1)
        else:
            @pl.loop(0, (planes - 2) // size)
            def _(group):
                some(group * size + 1)

        level.wait_x(step)
        face = one(0, level.z_send[step + 1])
        face = one(planes - 1, face)
        level.start(level.x_copies(step + 1))
        level.z_send[step + 1] = face
        level.start_yz(step + 1)

    for step in range(SWEEPS):
        sweep(fine, step, weight, scaled, bx)
        if step == 0:
            coarse.spread(0)
    store_fine = pltpu.make_async_copy(f_fields[SWEEPS].at[pl.ds(1, bx)], fine_hbm, local_sem.at[5])
    store_fine.start()

    fine.wait_yz(SWEEPS)

    def defect_pair(x):
        total = None
        for plane in (2 * x, 2 * x + 1):
            value, around = fine.around(SWEEPS, plane)
            part = rhs[plane] - ((6.0 + damp[plane]) * value - around)
            total = part if total is None else total + part
        halves[pl.ds(pl.multiple_of(x * by, by), by), :] = split_dot(total, pair_fine, (((1,), (0,)), ((), ())))

    @pl.loop(1, middle.nx - 1, unroll=2)
    def _(x):
        defect_pair(x)

    fine.wait_x(SWEEPS)
    defect_pair(0)
    defect_pair(middle.nx - 1)

    def enter(level, scratch, source, weights, scaleds):
        ny = level.ny
        face = jnp.zeros((ny, LANES), jnp.float32)
        for x in range(level.nx):
            even = scratch[pl.ds(x * 2 * ny, ny, stride=2), :]
            odd = scratch[pl.ds(x * 2 * ny + 1, ny, stride=2), :]
            source[x] = 0.5 * (even + odd)
            new = weights[x] * source[x]
            scaleds[x] = new
            level.fields[0][x + 1] = new
            face = level.pack(0, x, new, face)
        level.z_send[0] = face
        level.start_all(0)

    enter(middle, halves, m_src, m_weight, m_scaled)
    for step in range(SWEEPS - 1):
        sweep(middle, step, m_weight, m_scaled, middle.nx)
    last = SWEEPS - 1
    store_middle = pltpu.make_async_copy(m_fields[last].at[pl.ds(1, middle.nx)], middle_hbm, local_sem.at[6])
    store_middle.start()
    middle.wait_yz(last)
    middle.wait_x(last)

    my = middle.ny
    for x in range(coarse.nx):
        total = None
        for plane in (2 * x, 2 * x + 1):
            value, around = middle.around(last, plane)
            part = m_src[plane] - ((6.0 + m_damp[plane]) * value - around)
            total = part if total is None else total + part
        quarters[pl.ds(x * my, my), :] = split_dot(total, pair_middle, (((1,), (0,)), ((), ())))

    for x in range(coarse.nx):
        even = quarters[pl.ds(x * my, coarse.ny, stride=2), :]
        odd = quarters[pl.ds(x * my + 1, coarse.ny, stride=2), :]
        c_src[x] = 0.5 * (even + odd)
    coarse.merge(1, c_src[...])
    coarse.spread(1)
    coarse.collect(0)
    coarse.collect(1)
    coarse.smooth()
    for x in range(coarse.nx):
        c_out[x] = coarse.own(c_fields[last][coarse.nx + x])[:, :cells]
    store_coarse = pltpu.make_async_copy(c_out, coarse_hbm, local_sem.at[7])
    store_coarse.start()
    valid = lax.broadcasted_iota(jnp.int32, (coarse.ny, LANES), 1) < cells
    for x in range(coarse.nx):
        value, around = coarse.around(last, coarse.nx + x)
        part = c_src[x] - ((6.0 + c_damp[x]) * coarse.own(value) - coarse.own(around))
        c_defect[pl.ds(x * coarse.ny, coarse.ny), :] = jnp.where(valid, part, 0.0)

    packed = c_defect[pl.ds(0, rows // 2), :]
    packed = packed + pltpu.roll(c_defect[pl.ds(rows // 2, rows // 2), :], cells, 1)
    c_defect[pl.ds(0, rows // 2), :] = packed

    tall = NAGG // LANES

    def gather_row(row, total):
        number = lax.broadcasted_iota(jnp.int32, (tall, LANES), 0)
        parts = []
        for part in range(2):
            at = pl.ds(row + part * half, 1)
            high = group_rows[at, :] // LANES
            parts.append(jnp.where(number == high, c_defect[at, :], 0.0))
        values = jnp.concatenate(parts, axis=1)
        first = values.astype(jnp.bfloat16).astype(jnp.float32)
        both = jnp.concatenate([first, values - first], axis=0).astype(jnp.bfloat16)
        return total + lax.dot_general(both, onehot[row], (((1,), (1,)), ((), ())),
                                       preferred_element_type=jnp.float32)

    sums = lax.fori_loop(0, half, gather_row, jnp.zeros((2 * tall, LANES), jnp.float32),
                         unroll=4)
    mine = gx * cz + gz
    reduced[mine] = sums[:tall] + sums[tall:]

    def reduce_copy(i, k):
        return pltpu.make_async_remote_copy(
            src_ref=reduced.at[mine], dst_ref=reduced.at[mine],
            send_sem=r_send.at[i * cz + k], recv_sem=r_recv.at[mine],
            device_id=(i, gy, k), device_id_type=MESH)

    def reduce_wait(i, k):
        return pltpu.make_async_remote_copy(
            src_ref=reduced.at[i * cz + k], dst_ref=reduced.at[i * cz + k],
            send_sem=r_send.at[i * cz + k], recv_sem=r_recv.at[i * cz + k],
            device_id=(i, gy, k), device_id_type=MESH)

    def mates_do(act):
        for i, k in mates:
            pl.when(jnp.logical_or(gx != i, gz != k))(functools.partial(act, i, k))

    mates_do(lambda i, k: reduce_copy(i, k).start())
    mates_do(lambda i, k: reduce_wait(i, k).wait_recv())
    gathered[gy] = jnp.sum(reduced[...], axis=0)

    def gather_copy(j, slot, recv):
        return pltpu.make_async_remote_copy(
            src_ref=gathered.at[slot], dst_ref=gathered.at[slot],
            send_sem=g_send.at[j], recv_sem=g_recv.at[recv],
            device_id=(gx, j, gz), device_id_type=MESH)

    for j in range(cy):
        pl.when(gy != j)(lambda j=j: gather_copy(j, gy, gy).start())
    for j in range(cy):
        pl.when(gy != j)(lambda j=j: gather_copy(j, j, j).wait_recv())
    total_cells = rows * cells * cx * cy * cz
    source = jnp.sum(gathered[...], axis=0) * (1.0 / math.sqrt(total_cells // NAGG))

    loads[4].wait()
    out_rows = inverse.shape[0]
    product = None
    for part in range(tall):
        term = inverse[:, part * LANES:(part + 1) * LANES] * source[part:part + 1]
        product = term if product is None else product + term
    ones = jnp.ones((8, LANES), jnp.float32)
    solved = lax.dot_general(ones, product, (((1,), (1,)), ((), ())),
                             precision=lax.Precision.HIGHEST, preferred_element_type=jnp.float32)
    solved_ref[...] = solved[0:1]

    for step in range(SWEEPS + 1):
        if step == 0:
            fine.wait_send(first_x)
            fine.wait_send(fine.y_copies(0))
            fine.z_copy(0).wait_send()
        else:
            fine.wait_sends(step)
    for step in range(SWEEPS):
        middle.wait_sends(step)
    coarse.wait_sends()
    mates_do(lambda i, k: reduce_copy(i, k).wait_send())
    for j in range(cy):
        pl.when(gy != j)(lambda j=j: gather_copy(j, gy, gy).wait_send())
    store_fine.wait()
    store_middle.wait()
    store_coarse.wait()


def shards(counts, right_side, initial_guess, damping, group_map, block_inverse):
    bx, by, bz = right_side.shape
    f32 = jnp.float32
    vm = pltpu.VMEM

    def level_scratch(nx, ny, lanes, rounds):
        return [
            [vm((nx + 2, ny, lanes), f32)] * rounds,
            vm((rounds, 2, nx, lanes), f32), vm((rounds, 2, nx, lanes), f32),
            vm((rounds, ny, LANES), f32), vm((rounds, ny, LANES), f32),
        ]

    cx, cy, cz = counts
    mid = (bx // 2, by // 2, bz // 2)
    low = (bx // 4, by // 4, bz // 4)
    low_pad = (low[0], low[1], LANES)
    wide = (3 * low[0], low[1] + 2 * MARGIN, LANES)
    rows = low[0] * low[1]
    out_rows = block_inverse.shape[0]
    dma = pltpu.SemaphoreType.DMA
    any_space = pl.BlockSpec(memory_space=pl.ANY)
    in_hbm = pl.BlockSpec(memory_space=pltpu.HBM)
    outs = pl.pallas_call(
        functools.partial(kernel, counts),
        out_shape=(
            jax.ShapeDtypeStruct((bx, by, bz), f32),
            jax.ShapeDtypeStruct(mid, f32),
            jax.ShapeDtypeStruct(low, f32),
            jax.ShapeDtypeStruct((1, out_rows), f32),
        ),
        in_specs=[in_hbm] * 5,
        out_specs=(any_space, any_space, any_space, pl.BlockSpec(memory_space=pltpu.VMEM)),
        scratch_shapes=[
            *level_scratch(bx, by, bz, SWEEPS + 1),
            *level_scratch(*mid, SWEEPS),
            [vm(wide, f32)] * SWEEPS, vm((2, *wide), f32),
            vm((2, *low_pad), f32), vm((2, *low_pad), f32), vm((2, *low_pad), f32),
            vm((bx, by, bz), f32), vm((bx, by, bz), f32), vm(low, jnp.int32), vm(block_inverse.shape, f32),
            vm((bx, by, bz), f32), vm((bx, by, bz), f32),
            vm(mid, f32), vm(mid, f32), vm(mid, f32), vm(mid, f32),
            vm(low_pad, f32), vm(low_pad, f32),
            vm((mid[0] * by, LANES), f32), vm((low[0] * mid[1], LANES), f32),
            vm((rows, LANES), f32), vm(low, f32), vm((rows, LANES), jnp.int32),
            vm((rows // 4, LANES, 2 * LANES), jnp.bfloat16),
            vm((cx * cz, NAGG // LANES, LANES), f32), vm((cy, NAGG // LANES, LANES), f32),
            dma((SWEEPS + 1, 5)), dma((SWEEPS + 1, 5)),
            dma((SWEEPS, 5)), dma((SWEEPS, 5)), dma((2,)), dma((2,)), dma((2, 9)), dma((2, 9)),
            dma((cx * cz,)), dma((cx * cz,)), dma((cy,)), dma((cy,)), dma((8,)),
        ],
        compiler_params=pltpu.CompilerParams(
            collective_id=0, has_side_effects=True, vmem_limit_bytes=63 * 1024 * 1024),
        cost_estimate=pl.CostEstimate(flops=40_000_000, bytes_accessed=6_000_000, transcendentals=0),
    )(right_side, initial_guess, damping, group_map, block_inverse)
    fine, middle, coarse, solved = outs
    return fine, middle, coarse, solved.reshape(out_rows)


def solution(mesh):
    counts = tuple(mesh.shape[axis] for axis in ("gx", "gy", "gz"))
    cells = P("gx", "gy", "gz")
    return jax.shard_map(
        functools.partial(shards, counts),
        mesh=mesh,
        in_specs=(cells, cells, cells, cells, P("gy", None)),
        out_specs=(cells, cells, cells, P("gy")),
        check_vma=False,
    )
```
